256 devices in a mesh: ctx: 16 (over x_hi, z), tp: 16 (over y, x_lo, core).
Axes of the slice: x: 4 (x_hi: 2, x_lo: 2; x = x_hi * 2 + x_lo), y: 4, z: 8, core: 2. Of those that a mesh axis runs over, the one named last changes fastest.
Arguments:
- queries: bfloat16 [12288, 8192], P('ctx', 'tp'), may hold values from -6 to 6
- keys_in: bfloat16 [12288, 8192], P('ctx', 'tp'), may hold values from -6 to 6
- values_in: bfloat16 [12288, 8192], P('ctx', 'tp'), may hold values from -6 to 6
- short_taps: bfloat16 [3, 8192], P(None, 'tp'), may hold values from -3.5 to 3.5
- filters: bfloat16 [8192, 128], P('tp'), may hold values from -0.5 to 0.5
- skip_gain: float32 [8192], P('tp'), may hold values from -1 to 1
- out_weight: bfloat16 [8192, 8192], P('tp'), may hold values from -0.0625 to 0.0625
- residual: bfloat16 [12288, 8192], P(('ctx', 'tp')), may hold values from -6 to 6
Outputs:
- block_out: bfloat16 [12288, 8192], P(('ctx', 'tp'))
The draws below stay inside these ranges and needn't reach their ends.
All inputs are finite; a program needn't handle non-finite values.
Results may differ from the reference program's by a relative error of at most 0.022.
Values may be sent and summed in bfloat16 or wider, within the bound.
No kernel may reach another device: no remote copies, remote signals or barrier semaphores. Data moves between devices by JAX's collectives and lax.ppermute only.
A program may use at most 128 MiB of HBM per device.

```python
import jax
import jax.numpy as jnp
from jax import lax

D = 8192
LF = 128
KS = 3
TOKENS = 12288
N_TP = 16


def steps_of(rng, shape, split, low, top_value):
    loudness, own = 1.0, jax.random.fold_in(rng, 6)
    for position, shards_of in split:
        draws = jnp.exp(jax.random.uniform(jax.random.fold_in(own, position), (shards_of,), jnp.float32, low / len(split), top_value / len(split)))
        loudness = loudness * jnp.repeat(draws, shape[position] // shards_of).reshape([-1 if axis == position else 1 for axis in range(len(shape))])
    return loudness


def scatter_about(rng, dims, width, limit, cuts=(), dtype=jnp.bfloat16):
    loudness = steps_of(rng, dims, cuts, -0.22, 0.18) if cuts else 1.0
    array = jax.random.normal(rng, dims, jnp.float32) * width * loudness
    return jnp.minimum(jnp.maximum(array, -limit), limit).astype(dtype)


def setup_inputs(seed: int = 0) -> dict:
    streams_of = jax.random.split(jax.random.key(seed), 9)
    queries = scatter_about(streams_of[0], (TOKENS, D), 1.0, 6.0, ((0, 16), (1, 16)))
    keys_in = scatter_about(streams_of[1], (TOKENS, D), 1.0, 6.0, ((0, 16), (1, 16)))
    values_in = scatter_about(streams_of[2], (TOKENS, D), 1.0, 6.0, ((0, 16), (1, 16)))
    short_taps = scatter_about(streams_of[3], (KS, D), KS ** -0.5, 3.5, ((1, 16),))
    filters = scatter_about(streams_of[4], (D, LF), LF ** -0.5, 0.5, ((0, 16),))
    skip_gain = jnp.clip(jax.random.uniform(streams_of[5], (D,), jnp.float32, -1.0, 1.0) * steps_of(streams_of[5], (D,), ((0, 16),), -0.4, 0.0), -1.0, 1.0)
    out_weight = scatter_about(streams_of[6], (D, D), D ** -0.5, 0.0625, ((0, 16),))
    residual = scatter_about(streams_of[7], (TOKENS, D), 1.0, 6.0, ((0, 256),))
    return dict(queries=queries, keys_in=keys_in, values_in=values_in, short_taps=short_taps, filters=filters, skip_gain=skip_gain, out_weight=out_weight, residual=residual)


def featurize(sequence, tap_weights, out_rows):
    result = jnp.zeros((out_rows, sequence.shape[1]), jnp.float32)
    for offset in range(tap_weights.shape[0]):
        start = tap_weights.shape[0] - 1 - offset
        result = result + tap_weights[offset].astype(jnp.float32) * sequence[start:start + out_rows].astype(jnp.float32)
    return result


def reference(queries, keys_in, values_in, short_taps, filters, skip_gain, out_weight, residual):
    pad_rows = jnp.zeros((KS - 1, D), jnp.bfloat16)
    q_feat = featurize(jnp.concatenate([pad_rows, queries]), short_taps, TOKENS)
    k_feat = featurize(jnp.concatenate([pad_rows, keys_in]), short_taps, TOKENS)
    v_feat = featurize(jnp.concatenate([pad_rows, values_in]), short_taps, TOKENS)
    product = (k_feat * v_feat).astype(jnp.bfloat16)
    widened = jnp.concatenate([jnp.zeros((LF - 1, D), jnp.float32), product.astype(jnp.float32)])
    tap_table = filters.astype(jnp.float32)

    def add_tap(index_tap, accum):
        start = (LF - 1 - index_tap).astype(jnp.int32)
        window = lax.dynamic_slice_in_dim(widened, start, TOKENS, 0)
        column = lax.dynamic_slice_in_dim(tap_table, jnp.asarray(index_tap).astype(jnp.int32), 1, 1)[:, 0]
        return accum + column * window

    filtered = lax.fori_loop(0, LF, add_tap, jnp.zeros((TOKENS, D), jnp.float32))
    gated = (q_feat * (filtered + skip_gain * product.astype(jnp.float32))).astype(jnp.bfloat16)
    group_width = D // N_TP

    def add_group(index_group, accum):
        start = (index_group * group_width).astype(jnp.int32)
        columns = lax.dynamic_slice_in_dim(gated, start, group_width, 1)
        block = lax.dynamic_slice_in_dim(out_weight, start, group_width, 0)
        partial_sum = jnp.dot(columns, block, preferred_element_type=jnp.float32).astype(jnp.bfloat16)
        partial_sum = lax.optimization_barrier(partial_sum)
        return accum + partial_sum.astype(jnp.float32)

    summed = lax.fori_loop(0, N_TP, add_group, residual.astype(jnp.float32))
    return summed.astype(jnp.bfloat16)
```

```python
import math
import functools
import numpy as np
import jax
import jax.numpy as jnp
from jax import lax
from jax.experimental import pallas as pl
from jax.experimental.pallas import tpu as pltpu
from jax.sharding import PartitionSpec as P

BLK = 128
N_Y, N_X, N_C = 4, 2, 2


def split_bf16(matrix):
    high = matrix.astype(jnp.bfloat16)
    low = (matrix - high.astype(np.float64)).astype(jnp.bfloat16)
    return high, low


def transform_tables(taps):
    span = 2 * taps
    freq = np.arange(taps)[:, None] + 0.5
    time = np.arange(span)[None, :]
    angle = 2.0 * np.pi * freq * time / span
    forward = np.concatenate([np.cos(angle), -np.sin(angle)], axis=0)
    inverse = (2.0 / span) * forward.T[taps:]
    f_high, f_low = split_bf16(forward)
    g_high, g_low = split_bf16(inverse)
    return np.concatenate([f_high, f_low], axis=0), np.concatenate([g_high, g_low], axis=0)


def short_filter(window, taps):
    rows = window.shape[0] - 16
    wide = window.astype(jnp.float32)
    total = taps[0:1] * wide[16 : 16 + rows]
    for j in range(1, taps.shape[0]):
        total = total + taps[j : j + 1] * wide[16 - j : 16 - j + rows]
    return total


def gate_kernel(place_ref, order_ref, q_ref, k_ref, v_ref, halo_ref, taps_ref, filt_ref, skip_ref, f_ref, g_ref, keep_ref, give_ref, prod_ref, gated_ref):
    rows = q_ref.shape[0]
    blocks = rows // BLK
    taps = taps_ref[...].astype(jnp.float32)
    skip = skip_ref[...]
    tail = BLK + 16

    def window(ref, base, b):
        if b == 0:
            return halo_ref[base : base + tail]
        if b == 1:
            return jnp.concatenate([halo_ref[base + BLK : base + tail], ref[0:BLK]], axis=0)
        return ref[(b - 1) * BLK - 16 : b * BLK]

    spec = lax.dot_general(
        f_ref[:, :BLK], filt_ref[...], (((1,), (1,)), ((), ())), preferred_element_type=jnp.float32
    )
    spec = spec[: 2 * BLK] + spec[2 * BLK :]
    h_re, h_im = spec[:BLK], spec[BLK:]
    for b in range(blocks + 1):
        prod = short_filter(window(k_ref, 16, b), taps) * short_filter(window(v_ref, 16 + tail, b), taps)
        prod_ref[b * BLK : (b + 1) * BLK] = prod.astype(jnp.bfloat16)
        if b == 0:
            continue
        x = jnp.dot(f_ref[...], prod_ref[(b - 1) * BLK : (b + 1) * BLK], preferred_element_type=jnp.float32)
        x = x[: 2 * BLK] + x[2 * BLK :]
        x_re, x_im = x[:BLK], x[BLK:]
        y = jnp.concatenate([x_re * h_re - x_im * h_im, x_re * h_im + x_im * h_re], axis=0)
        y_high = y.astype(jnp.bfloat16)
        y_low = (y - y_high.astype(jnp.float32)).astype(jnp.bfloat16)
        z = jnp.dot(g_ref[...], y_high, preferred_element_type=jnp.float32)
        z = z[:BLK] + z[BLK:] + jnp.dot(g_ref[:BLK], y_low, preferred_element_type=jnp.float32)
        own = prod_ref[b * BLK : (b + 1) * BLK].astype(jnp.float32)
        if b == 1:
            q_win = jnp.concatenate([halo_ref[0:16], q_ref[0:BLK]], axis=0)
        else:
            q_win = q_ref[(b - 1) * BLK - 16 : b * BLK]
        gated = short_filter(q_win, taps) * (z + skip * own)
        gated_ref[(b - 1) * BLK : b * BLK] = gated.astype(jnp.bfloat16)

    slots = N_Y * N_X
    piece = keep_ref.shape[0] // slots
    for slot in range(slots):
        for which, ref in ((0, keep_ref), (1, give_ref)):
            group = order_ref[(place_ref[0] * 2 + which) * slots + slot]
            start = pl.multiple_of(group * piece, 16)
            ref[slot * piece : (slot + 1) * piece] = gated_ref[pl.ds(start, piece)]


def row_order():
    table = []
    for y in range(N_Y):
        for x in range(N_X):
            for c in range(N_C):
                for dc in range(N_C):
                    for dx in range(N_X):
                        for dy in range(N_Y):
                            table.append((((y + dy) % N_Y) * N_X + (x + dx) % N_X) * N_C + (c + dc) % N_C)
    return np.array(table, np.int32)


def gate(place, queries, keys_in, values_in, halo, short_taps, filters, skip_gain):
    rows, channels = queries.shape
    width = 256
    f_tab, g_tab = transform_tables(filters.shape[1])
    col = lambda i, *_: (0, i)
    fixed = lambda i, *_: (0, 0)
    half = jax.ShapeDtypeStruct((rows // 2, channels), jnp.bfloat16)
    return pl.pallas_call(
        gate_kernel,
        grid_spec=pltpu.PrefetchScalarGridSpec(
            num_scalar_prefetch=2,
            grid=(channels // width,),
            in_specs=[
                pl.BlockSpec((rows, width), col),
                pl.BlockSpec((rows, width), col),
                pl.BlockSpec((rows, width), col),
                pl.BlockSpec((halo.shape[0], width), col),
                pl.BlockSpec((short_taps.shape[0], width), col),
                pl.BlockSpec((width, filters.shape[1]), lambda i, *_: (i, 0)),
                pl.BlockSpec((1, width), col),
                pl.BlockSpec(f_tab.shape, fixed),
                pl.BlockSpec(g_tab.shape, fixed),
            ],
            out_specs=[pl.BlockSpec((rows // 2, width), col)] * 2,
            scratch_shapes=[
                pltpu.VMEM((rows + BLK, width), jnp.bfloat16),
                pltpu.VMEM((rows, width), jnp.bfloat16),
            ],
        ),
        out_shape=[half, half],
        compiler_params=pltpu.CompilerParams(vmem_limit_bytes=32 * 1024 * 1024),
        cost_estimate=pl.CostEstimate(flops=6 * 10**9, bytes_accessed=4 * 10**6, transcendentals=0),
        name="gate",
    )(place, jnp.asarray(row_order()), queries, keys_in, values_in, halo, short_taps, filters, skip_gain[None, :], f_tab, g_tab)


TILE = 256


def project_kernel(pieces, a_ref, b_ref, wa_ref, wb_ref, *out_refs):
    acc = jnp.dot(a_ref[...], wa_ref[...], preferred_element_type=jnp.float32)
    acc = acc + jnp.dot(b_ref[...], wb_ref[...], preferred_element_type=jnp.float32)
    acc = acc.astype(jnp.bfloat16)
    for ref, spans in zip(out_refs, pieces):
        at = 0
        for start, stop in spans:
            ref[at : at + stop - start] = acc[start:stop]
            at += stop - start


def project(mine, theirs, weight, weight_pair, first, count, pieces):
    rows, depth = mine.shape
    sizes = [sum(stop - start for start, stop in spans) for spans in pieces]
    lhs = pl.BlockSpec((rows, depth), lambda j: (0, 0))
    rhs = pl.BlockSpec((depth, TILE), lambda j: (0, j + first // TILE))
    return pl.pallas_call(
        functools.partial(project_kernel, pieces),
        grid=(count // TILE,),
        out_shape=[jax.ShapeDtypeStruct((n, count), jnp.bfloat16) for n in sizes],
        in_specs=[lhs, lhs, rhs, rhs],
        out_specs=[pl.BlockSpec((n, TILE), lambda j: (0, j)) for n in sizes],
        compiler_params=pltpu.CompilerParams(vmem_limit_bytes=32 * 1024 * 1024),
        cost_estimate=pl.CostEstimate(
            flops=4 * rows * depth * count, bytes_accessed=2 * (2 * depth + rows) * count, transcendentals=0
        ),
        name="project",
    )(mine, theirs, weight, weight_pair)


def moved(dy=0, dx=0, dc=0):
    pairs = []
    for y in range(N_Y):
        for x in range(N_X):
            for c in range(N_C):
                source = (y * N_X + x) * N_C + c
                target = (((y + dy) % N_Y) * N_X + (x + dx) % N_X) * N_C + (c + dc) % N_C
                pairs.append((source, target))
    return pairs


def send(array, **step):
    return lax.ppermute(array, "tp", moved(**step))


def add(*arrays):
    total = arrays[0].astype(jnp.float32)
    for array in arrays[1:]:
        total = total + array.astype(jnp.float32)
    return total


def reduce_y(first, second):
    far_second = send(second[2], dy=1)
    far_first = send(first[2], dy=-1)
    up_first = send(first[1], dy=1)
    down_second = send(second[3], dy=-1)
    up_second = send(add(second[1], far_second).astype(jnp.bfloat16), dy=1)
    down_first = send(add(first[3], far_first).astype(jnp.bfloat16), dy=-1)
    return add(first[0], up_first, down_first), add(second[0], down_second, up_second)


X_FIRST = 1792


def body(queries, keys_in, values_in, short_taps, filters, skip_gain, out_weight, residual):
    rows = queries.shape[0]
    width = out_weight.shape[1]
    tail = filters.shape[1] + 16
    peers = lax.axis_size("ctx")
    piece = rows // (N_Y * N_X * N_C)
    weight_pair = send(out_weight, dc=1)
    rim = jnp.concatenate([queries[rows - 16 :], keys_in[rows - tail :], values_in[rows - tail :]])
    halo = lax.ppermute(rim, "ctx", [(i, i + 1) for i in range(peers - 1)])

    place = lax.axis_index("tp").astype(jnp.int32)[None]
    keep, give = gate(place, queries, keys_in, values_in, halo, short_taps, filters, skip_gain)
    theirs = send(give, dc=1)

    half = rows // (2 * N_C)
    by_x = (((0, half),), ((half, 2 * half),))
    by_y = tuple(((s * piece, (s + 1) * piece), (half + s * piece, half + (s + 1) * piece)) for s in range(N_Y))
    y_first = width // 2 - X_FIRST
    multiply = functools.partial(project, keep, theirs, out_weight, weight_pair)
    a0_keep, a0_give = multiply(0, X_FIRST, by_x)
    a0_got = send(a0_give, dx=1)
    b0 = multiply(2 * X_FIRST, y_first, by_y)
    b1 = multiply(2 * X_FIRST + y_first, y_first, by_y)
    a1_keep, a1_give = multiply(X_FIRST, X_FIRST, by_x)
    a1_got = send(a1_give, dx=1)

    b0_sum, b1_sum = reduce_y(b0, b1)
    b0_got = send(b0_sum[piece:].astype(jnp.bfloat16), dx=1)
    b1_got = send(b1_sum[piece:].astype(jnp.bfloat16), dx=1)

    def sections(keep_part, got):
        total = add(keep_part, got)
        return [total[: piece]] + [total[s * piece : (s + 1) * piece].astype(jnp.bfloat16) for s in range(1, N_Y)]

    a0_sum, a1_sum = reduce_y(sections(a0_keep, a0_got), sections(a1_keep, a1_got))
    summed = jnp.concatenate(
        [a0_sum, a1_sum, add(b0_sum[:piece], b0_got), add(b1_sum[:piece], b1_got)], axis=1
    )
    return (residual.astype(jnp.float32) + summed).astype(jnp.bfloat16)


def solution(mesh):
    in_specs = (
        P("ctx", "tp"),
        P("ctx", "tp"),
        P("ctx", "tp"),
        P(None, "tp"),
        P("tp", None),
        P("tp"),
        P("tp", None),
        P(("ctx", "tp"), None),
    )
    out_specs = P(("ctx", "tp"), None)
    return jax.shard_map(body, mesh=mesh, in_specs=in_specs, out_specs=out_specs, check_vma=False)
```

```python
import math
import functools
import numpy as np
import jax
import jax.numpy as jnp
from jax import lax
from jax.experimental import pallas as pl
from jax.experimental.pallas import tpu as pltpu
from jax.sharding import PartitionSpec as P

BLK = 128
N_Y, N_X, N_C = 4, 2, 2


def split_bf16(matrix):
    high = matrix.astype(jnp.bfloat16)
    low = (matrix - high.astype(np.float64)).astype(jnp.bfloat16)
    return high, low


def transform_tables(taps):
    span = 2 * taps
    freq = np.arange(taps)[:, None] + 0.5
    time = np.arange(span)[None, :]
    angle = 2.0 * np.pi * freq * time / span
    forward = np.concatenate([np.cos(angle), -np.sin(angle)], axis=0)
    inverse = (2.0 / span) * forward.T[taps:]
    f_high, f_low = split_bf16(forward)
    g_high, g_low = split_bf16(inverse)
    return np.concatenate([f_high, f_low], axis=0), np.concatenate([g_high, g_low], axis=0)


def short_filter(wide, taps):
    rows = wide.shape[0] - 16
    total = taps[0:1] * wide[16 : 16 + rows]
    for j in range(1, taps.shape[0]):
        total = total + taps[j : j + 1] * wide[16 - j : 16 - j + rows]
    return total


def spectrum(f_ref, filt_ref):
    spec = lax.dot_general(
        f_ref[:, :BLK], filt_ref[...], (((1,), (1,)), ((), ())), preferred_element_type=jnp.float32
    )
    spec = spec[: 2 * BLK] + spec[2 * BLK :]
    return spec[:BLK], spec[BLK:]


def long_filter(span, h_re, h_im, f_ref, g_ref):
    x = jnp.dot(f_ref[...], span, preferred_element_type=jnp.float32)
    x = x[: 2 * BLK] + x[2 * BLK :]
    x_re, x_im = x[:BLK], x[BLK:]
    y = jnp.concatenate([x_re * h_re - x_im * h_im, x_re * h_im + x_im * h_re], axis=0)
    y_high = y.astype(jnp.bfloat16)
    y_low = (y - y_high.astype(jnp.float32)).astype(jnp.bfloat16)
    z = jnp.dot(g_ref[...], y_high, preferred_element_type=jnp.float32)
    return z[:BLK] + z[BLK:] + jnp.dot(g_ref[:BLK], y_low, preferred_element_type=jnp.float32)


def window(ref, b):
    return ref[b * BLK - 16 : (b + 1) * BLK].astype(jnp.float32)


def rim_kernel(q_ref, k_ref, v_ref, taps_ref, out_ref):
    taps = taps_ref[...].astype(jnp.float32)
    tail = BLK + 16
    at = k_ref.shape[0] - tail
    k_win, v_win = k_ref[at:].astype(jnp.float32), v_ref[at:].astype(jnp.float32)
    out_ref[:BLK] = (short_filter(k_win, taps) * short_filter(v_win, taps)).astype(jnp.bfloat16)
    q_end = pltpu.roll(q_ref[...].astype(jnp.float32), 2, 0)
    k_end = pltpu.roll(k_win[BLK:], 4, 0)
    v_end = pltpu.roll(v_win[BLK:], 6, 0)
    row = lax.broadcasted_iota(jnp.int32, q_end.shape, 0)
    packed = jnp.where(row < 2, q_end, jnp.where(row < 4, k_end, v_end))
    out_ref[BLK:] = packed.astype(jnp.bfloat16)


def late_kernel(first, q_ref, k_ref, v_ref, taps_ref, filt_ref, skip_ref, f_ref, g_ref, out_ref, prod_ref):
    blocks = q_ref.shape[0] // BLK
    taps = taps_ref[...].astype(jnp.float32)
    skip = skip_ref[...]
    h_re, h_im = spectrum(f_ref, filt_ref)
    for b in range(first - 1, blocks):
        at = (b - first + 1) * BLK
        prod = short_filter(window(k_ref, b), taps) * short_filter(window(v_ref, b), taps)
        prod = prod.astype(jnp.bfloat16)
        prod_ref[at : at + BLK] = prod
        if b >= first:
            filtered = long_filter(prod_ref[at - BLK : at + BLK], h_re, h_im, f_ref, g_ref)
            gated = short_filter(window(q_ref, b), taps) * (filtered + skip * prod.astype(jnp.float32))
            out_ref[at - BLK : at] = gated.astype(jnp.bfloat16)


def early_kernel(
    place_ref, order_ref, q_ref, k_ref, v_ref, halo_ref, late_ref, taps_ref, filt_ref, skip_ref, f_ref, g_ref,
    keep_ref, give_ref, prod_ref, gated_ref,
):
    blocks = q_ref.shape[0] // BLK
    taps = taps_ref[...].astype(jnp.float32)
    skip = skip_ref[...]
    rim = halo_ref[BLK:].astype(jnp.float32)

    def rows_of(ref, b, turn):
        if b == 0:
            return jnp.concatenate([pltpu.roll(rim, turn, 0), ref[:BLK].astype(jnp.float32)], axis=0)
        return window(ref, b)

    h_re, h_im = spectrum(f_ref, filt_ref)
    prod_ref[:BLK] = halo_ref[:BLK]
    for b in range(blocks):
        prod = short_filter(rows_of(k_ref, b, 12), taps) * short_filter(rows_of(v_ref, b, 10), taps)
        prod = prod.astype(jnp.bfloat16)
        prod_ref[(b + 1) * BLK : (b + 2) * BLK] = prod
        filtered = long_filter(prod_ref[b * BLK : (b + 2) * BLK], h_re, h_im, f_ref, g_ref)
        gated = short_filter(rows_of(q_ref, b, 14), taps) * (filtered + skip * prod.astype(jnp.float32))
        gated_ref[b * BLK : (b + 1) * BLK] = gated.astype(jnp.bfloat16)
    gated_ref[blocks * BLK :] = late_ref[...]

    slots = N_Y * N_X
    piece = keep_ref.shape[0] // slots
    for slot in range(slots):
        for which, ref in ((0, keep_ref), (1, give_ref)):
            group = order_ref[(place_ref[0] * 2 + which) * slots + slot]
            start = pl.multiple_of(group * piece, 16)
            ref[slot * piece : (slot + 1) * piece] = gated_ref[pl.ds(start, piece)]


def row_order():
    table = []
    for y in range(N_Y):
        for x in range(N_X):
            for c in range(N_C):
                for dc in range(N_C):
                    for dx in range(N_X):
                        for dy in range(N_Y):
                            table.append((((y + dy) % N_Y) * N_X + (x + dx) % N_X) * N_C + (c + dc) % N_C)
    return np.array(table, np.int32)


VMEM_LIMIT = 24 * 1024 * 1024
EARLY = 2
WIDTH = 256


def stay(array):
    return pltpu.with_memory_space_constraint(array, pltpu.HBM)


def column_block(rows, index=0):
    return pl.BlockSpec((rows, WIDTH), lambda i, *_: (index, i))


def whole(shape):
    return pl.BlockSpec(shape, lambda i, *_: (0, 0))


def make_rim(queries, keys_in, values_in, short_taps):
    rows, channels = queries.shape
    part = rows // 4
    return pl.pallas_call(
        rim_kernel,
        grid=(channels // WIDTH,),
        out_shape=jax.ShapeDtypeStruct((BLK + 16, channels), jnp.bfloat16),
        in_specs=[
            column_block(16, rows // 16 - 1),
            column_block(part, rows // part - 1),
            column_block(part, rows // part - 1),
            column_block(short_taps.shape[0]),
        ],
        out_specs=column_block(BLK + 16),
        compiler_params=pltpu.CompilerParams(vmem_limit_bytes=VMEM_LIMIT),
        cost_estimate=pl.CostEstimate(flops=10**9, bytes_accessed=10**6, transcendentals=0),
        name="rim",
    )(stay(queries), stay(keys_in), stay(values_in), stay(short_taps))


def parameter_specs(short_taps, filters, tables):
    return [
        column_block(short_taps.shape[0]),
        pl.BlockSpec((WIDTH, filters.shape[1]), lambda i, *_: (i, 0)),
        column_block(1),
        whole(tables[0].shape),
        whole(tables[1].shape),
    ]


def gate_late(queries, keys_in, values_in, short_taps, filters, skip_gain, tables):
    rows, channels = queries.shape
    out_rows = rows - EARLY * BLK
    return pl.pallas_call(
        functools.partial(late_kernel, EARLY),
        grid=(channels // WIDTH,),
        out_shape=jax.ShapeDtypeStruct((out_rows, channels), jnp.bfloat16),
        in_specs=[column_block(rows)] * 3 + parameter_specs(short_taps, filters, tables),
        out_specs=column_block(out_rows),
        scratch_shapes=[pltpu.VMEM((out_rows + BLK, WIDTH), jnp.bfloat16)],
        compiler_params=pltpu.CompilerParams(vmem_limit_bytes=VMEM_LIMIT),
        cost_estimate=pl.CostEstimate(flops=4 * 10**9, bytes_accessed=3 * 10**6, transcendentals=0),
        name="gate_late",
    )(*map(stay, (queries, keys_in, values_in, short_taps, filters, skip_gain, *tables)))


def gate_early(place, queries, keys_in, values_in, halo, late, short_taps, filters, skip_gain, tables):
    rows, channels = queries.shape
    half = jax.ShapeDtypeStruct((rows // 2, channels), jnp.bfloat16)
    return pl.pallas_call(
        early_kernel,
        grid_spec=pltpu.PrefetchScalarGridSpec(
            num_scalar_prefetch=2,
            grid=(channels // WIDTH,),
            in_specs=[column_block(EARLY * BLK)] * 3
            + [column_block(halo.shape[0]), column_block(late.shape[0])]
            + parameter_specs(short_taps, filters, tables),
            out_specs=[column_block(rows // 2)] * 2,
            scratch_shapes=[
                pltpu.VMEM(((EARLY + 1) * BLK, WIDTH), jnp.bfloat16),
                pltpu.VMEM((rows, WIDTH), jnp.bfloat16),
            ],
        ),
        out_shape=[half, half],
        compiler_params=pltpu.CompilerParams(vmem_limit_bytes=VMEM_LIMIT),
        cost_estimate=pl.CostEstimate(flops=2 * 10**9, bytes_accessed=3 * 10**6, transcendentals=0),
        name="gate_early",
    )(
        place,
        jnp.asarray(row_order()),
        *map(stay, (queries, keys_in, values_in)),
        halo,
        late,
        *map(stay, (short_taps, filters, skip_gain, *tables)),
    )


def project_kernel(first, count, tile, pieces, a_ref, b_ref, wa_ref, wb_ref, *out_refs):
    depth = wa_ref.shape[0]

    def step(wa, wb, *outs):
        acc = jnp.dot(a_ref[...], wa[...], preferred_element_type=jnp.float32)
        acc = acc + jnp.dot(b_ref[...], wb[...], preferred_element_type=jnp.float32)
        acc = acc.astype(jnp.bfloat16)
        for ref, spans in zip(outs, pieces):
            at = 0
            for start, stop in spans:
                ref[at : at + stop - start] = acc[start:stop]
                at += stop - start

    rhs = pl.BlockSpec((depth, tile), lambda j: (0, j))
    pltpu.emit_pipeline(
        step,
        grid=(count // tile,),
        in_specs=[rhs, rhs],
        out_specs=[pl.BlockSpec((ref.shape[0], tile), lambda j: (0, j)) for ref in out_refs],
    )(wa_ref.at[:, pl.ds(first, count)], wb_ref.at[:, pl.ds(first, count)], *out_refs)


def project(mine, theirs, weight, weight_pair, first, count, tile, pieces):
    rows, depth = mine.shape
    sizes = [sum(stop - start for start, stop in spans) for spans in pieces]
    anywhere = pl.BlockSpec(memory_space=pl.ANY)
    return pl.pallas_call(
        functools.partial(project_kernel, first, count, tile, pieces),
        out_shape=[jax.ShapeDtypeStruct((n, count), jnp.bfloat16) for n in sizes],
        in_specs=[pl.BlockSpec(memory_space=pltpu.VMEM)] * 2 + [pl.BlockSpec(memory_space=pltpu.HBM)] * 2,
        out_specs=[anywhere] * len(sizes),
        compiler_params=pltpu.CompilerParams(vmem_limit_bytes=VMEM_LIMIT),
        cost_estimate=pl.CostEstimate(
            flops=4 * rows * depth * count, bytes_accessed=2 * (2 * depth + rows) * count, transcendentals=0
        ),
        name="project",
    )(mine, theirs, stay(weight), stay(weight_pair))


def moved(dy=0, dx=0, dc=0):
    pairs = []
    for y in range(N_Y):
        for x in range(N_X):
            for c in range(N_C):
                source = (y * N_X + x) * N_C + c
                target = (((y + dy) % N_Y) * N_X + (x + dx) % N_X) * N_C + (c + dc) % N_C
                pairs.append((source, target))
    return pairs


def send(array, **step):
    return lax.ppermute(array, "tp", moved(**step))


def add(*arrays):
    total = arrays[0].astype(jnp.float32)
    for array in arrays[1:]:
        total = total + array.astype(jnp.float32)
    return total


def reduce_y(first, second):
    far_second = send(second[2], dy=1)
    far_first = send(first[2], dy=-1)
    up_first = send(first[1], dy=1)
    down_second = send(second[3], dy=-1)
    up_second = send(add(second[1], far_second).astype(jnp.bfloat16), dy=1)
    down_first = send(add(first[3], far_first).astype(jnp.bfloat16), dy=-1)
    return add(first[0], up_first, down_first), add(second[0], down_second, up_second)


X_FIRST = 1792


def body(queries, keys_in, values_in, short_taps, filters, skip_gain, out_weight, residual):
    rows = queries.shape[0]
    width = out_weight.shape[1]
    peers = lax.axis_size("ctx")
    piece = rows // (N_Y * N_X * N_C)
    weight_pair = send(out_weight, dc=1)
    rim = make_rim(queries, keys_in, values_in, short_taps)
    halo = lax.ppermute(rim, "ctx", [(i, i + 1) for i in range(peers - 1)])
    parameters = (short_taps, filters, skip_gain[None, :], transform_tables(filters.shape[1]))
    late = gate_late(queries, keys_in, values_in, *parameters)
    place = lax.axis_index("tp").astype(jnp.int32)[None]
    keep, give = gate_early(place, queries, keys_in, values_in, halo, late, *parameters)
    theirs = send(give, dc=1)

    half = rows // (2 * N_C)
    by_x = (((0, half),), ((half, 2 * half),))
    by_y = tuple(((s * piece, (s + 1) * piece), (half + s * piece, half + (s + 1) * piece)) for s in range(N_Y))
    y_first = width // 2 - X_FIRST

    def multiply(after, *where):
        left = lax.optimization_barrier((keep, after))[0]
        return project(left, theirs, out_weight, weight_pair, *where)

    a0_keep, a0_give = multiply(place, 0, X_FIRST, X_FIRST // 2, by_x)
    a0_got = send(a0_give, dx=1)
    b0 = multiply(a0_keep, 2 * X_FIRST, y_first, y_first // 3, by_y)
    b1 = multiply(b0[0], 2 * X_FIRST + y_first, y_first, y_first // 3, by_y)
    a1_keep, a1_give = multiply(b1[0], X_FIRST, X_FIRST, X_FIRST // 2, by_x)
    a1_got = send(a1_give, dx=1)

    b0_sum, b1_sum = reduce_y(b0, b1)
    b0_got = send(b0_sum[piece:].astype(jnp.bfloat16), dx=1)
    b1_got = send(b1_sum[piece:].astype(jnp.bfloat16), dx=1)

    def sections(keep_part, got):
        total = add(keep_part, got)
        return [total[: piece]] + [total[s * piece : (s + 1) * piece].astype(jnp.bfloat16) for s in range(1, N_Y)]

    a0_sum, a1_sum = reduce_y(sections(a0_keep, a0_got), sections(a1_keep, a1_got))
    summed = jnp.concatenate(
        [a0_sum, a1_sum, add(b0_sum[:piece], b0_got), add(b1_sum[:piece], b1_got)], axis=1
    )
    return (residual.astype(jnp.float32) + summed).astype(jnp.bfloat16)


def solution(mesh):
    in_specs = (
        P("ctx", "tp"),
        P("ctx", "tp"),
        P("ctx", "tp"),
        P(None, "tp"),
        P("tp", None),
        P("tp"),
        P("tp", None),
        P(("ctx", "tp"), None),
    )
    out_specs = P(("ctx", "tp"), None)
    return jax.shard_map(body, mesh=mesh, in_specs=in_specs, out_specs=out_specs, check_vma=False)
```

```python
import math
import functools
import numpy as np
import jax
import jax.numpy as jnp
from jax import lax
from jax.experimental import pallas as pl
from jax.experimental.pallas import tpu as pltpu
from jax.sharding import PartitionSpec as P

BLK = 128
N_Y, N_X, N_C = 4, 2, 2


def split_bf16(matrix):
    high = matrix.astype(jnp.bfloat16)
    low = (matrix - high.astype(np.float64)).astype(jnp.bfloat16)
    return high, low


def transform_tables(taps):
    span = 2 * taps
    freq = np.arange(taps)[:, None] + 0.5
    time = np.arange(span)[None, :]
    angle = 2.0 * np.pi * freq * time / span
    forward = np.concatenate([np.cos(angle), -np.sin(angle)], axis=0)
    inverse = (2.0 / span) * forward.T[taps:]
    f_high, f_low = split_bf16(forward)
    g_high, g_low = split_bf16(inverse)
    return np.concatenate([f_high, f_low], axis=0), np.concatenate([g_high, g_low], axis=0)


def short_filter(wide, taps):
    rows = wide.shape[0] - 16
    total = taps[0:1] * wide[16 : 16 + rows]
    for j in range(1, taps.shape[0]):
        total = total + taps[j : j + 1] * wide[16 - j : 16 - j + rows]
    return total


def spectrum(f_ref, filt_ref):
    spec = lax.dot_general(
        f_ref[:, :BLK], filt_ref[...], (((1,), (1,)), ((), ())), preferred_element_type=jnp.float32
    )
    spec = spec[: 2 * BLK] + spec[2 * BLK :]
    return spec[:BLK], spec[BLK:]


def long_filter(span, h_re, h_im, f_ref, g_ref):
    x = jnp.dot(f_ref[...], span, preferred_element_type=jnp.float32)
    x = x[: 2 * BLK] + x[2 * BLK :]
    x_re, x_im = x[:BLK], x[BLK:]
    y = jnp.concatenate([x_re * h_re - x_im * h_im, x_re * h_im + x_im * h_re], axis=0)
    y_high = y.astype(jnp.bfloat16)
    y_low = (y - y_high.astype(jnp.float32)).astype(jnp.bfloat16)
    z = jnp.dot(g_ref[...], y_high, preferred_element_type=jnp.float32)
    return z[:BLK] + z[BLK:] + jnp.dot(g_ref[:BLK], y_low, preferred_element_type=jnp.float32)


def window(ref, b):
    return ref[b * BLK - 16 : (b + 1) * BLK].astype(jnp.float32)


def rim_kernel(q_ref, k_ref, v_ref, taps_ref, out_ref):
    taps = taps_ref[...].astype(jnp.float32)
    tail = BLK + 16
    at = k_ref.shape[0] - tail
    k_win, v_win = k_ref[at:].astype(jnp.float32), v_ref[at:].astype(jnp.float32)
    out_ref[:BLK] = (short_filter(k_win, taps) * short_filter(v_win, taps)).astype(jnp.bfloat16)
    q_end = pltpu.roll(q_ref[...].astype(jnp.float32), 2, 0)
    k_end = pltpu.roll(k_win[BLK:], 4, 0)
    v_end = pltpu.roll(v_win[BLK:], 6, 0)
    row = lax.broadcasted_iota(jnp.int32, q_end.shape, 0)
    packed = jnp.where(row < 2, q_end, jnp.where(row < 4, k_end, v_end))
    out_ref[BLK:] = packed.astype(jnp.bfloat16)


def late_kernel(first, q_ref, k_ref, v_ref, taps_ref, filt_ref, skip_ref, f_ref, g_ref, out_ref, prod_ref):
    blocks = q_ref.shape[0] // BLK
    taps = taps_ref[...].astype(jnp.float32)
    skip = skip_ref[...]
    h_re, h_im = spectrum(f_ref, filt_ref)
    for b in range(first - 1, blocks):
        at = (b - first + 1) * BLK
        prod = short_filter(window(k_ref, b), taps) * short_filter(window(v_ref, b), taps)
        prod = prod.astype(jnp.bfloat16)
        prod_ref[at : at + BLK] = prod
        if b >= first:
            filtered = long_filter(prod_ref[at - BLK : at + BLK], h_re, h_im, f_ref, g_ref)
            gated = short_filter(window(q_ref, b), taps) * (filtered + skip * prod.astype(jnp.float32))
            out_ref[at - BLK : at] = gated.astype(jnp.bfloat16)


def early_kernel(
    place_ref, order_ref, q_ref, k_ref, v_ref, halo_ref, late_ref, taps_ref, filt_ref, skip_ref, f_ref, g_ref,
    keep_ref, give_ref, prod_ref, gated_ref,
):
    blocks = q_ref.shape[0] // BLK
    taps = taps_ref[...].astype(jnp.float32)
    skip = skip_ref[...]
    rim = halo_ref[BLK:].astype(jnp.float32)

    def rows_of(ref, b, turn):
        if b == 0:
            return jnp.concatenate([pltpu.roll(rim, turn, 0), ref[:BLK].astype(jnp.float32)], axis=0)
        return window(ref, b)

    h_re, h_im = spectrum(f_ref, filt_ref)
    prod_ref[:BLK] = halo_ref[:BLK]
    for b in range(blocks):
        prod = short_filter(rows_of(k_ref, b, 12), taps) * short_filter(rows_of(v_ref, b, 10), taps)
        prod = prod.astype(jnp.bfloat16)
        prod_ref[(b + 1) * BLK : (b + 2) * BLK] = prod
        filtered = long_filter(prod_ref[b * BLK : (b + 2) * BLK], h_re, h_im, f_ref, g_ref)
        gated = short_filter(rows_of(q_ref, b, 14), taps) * (filtered + skip * prod.astype(jnp.float32))
        gated_ref[b * BLK : (b + 1) * BLK] = gated.astype(jnp.bfloat16)
    gated_ref[blocks * BLK :] = late_ref[...]

    slots = N_Y * N_X
    piece = keep_ref.shape[0] // slots
    for slot in range(slots):
        for which, ref in ((0, keep_ref), (1, give_ref)):
            group = order_ref[(place_ref[0] * 2 + which) * slots + slot]
            start = pl.multiple_of(group * piece, 16)
            ref[slot * piece : (slot + 1) * piece] = gated_ref[pl.ds(start, piece)]


def row_order():
    table = []
    for y in range(N_Y):
        for x in range(N_X):
            for c in range(N_C):
                for dc in range(N_C):
                    for dx in range(N_X):
                        for dy in range(N_Y):
                            table.append((((y + dy) % N_Y) * N_X + (x + dx) % N_X) * N_C + (c + dc) % N_C)
    return np.array(table, np.int32)


VMEM_LIMIT = 24 * 1024 * 1024
EARLY = 2
WIDTH = 256


def stay(array):
    return pltpu.with_memory_space_constraint(array, pltpu.HBM)


def column_block(rows, index=0):
    return pl.BlockSpec((rows, WIDTH), lambda i, *_: (index, i))


def whole(shape):
    return pl.BlockSpec(shape, lambda i, *_: (0, 0))


def make_rim(queries, keys_in, values_in, short_taps):
    rows, channels = queries.shape
    part = rows // 4
    return pl.pallas_call(
        rim_kernel,
        grid=(channels // WIDTH,),
        out_shape=jax.ShapeDtypeStruct((BLK + 16, channels), jnp.bfloat16),
        in_specs=[
            column_block(16, rows // 16 - 1),
            column_block(part, rows // part - 1),
            column_block(part, rows // part - 1),
            column_block(short_taps.shape[0]),
        ],
        out_specs=column_block(BLK + 16),
        compiler_params=pltpu.CompilerParams(vmem_limit_bytes=VMEM_LIMIT),
        cost_estimate=pl.CostEstimate(flops=10**9, bytes_accessed=10**6, transcendentals=0),
        name="rim",
    )(stay(queries), stay(keys_in), stay(values_in), stay(short_taps))


def parameter_specs(short_taps, filters, tables):
    return [
        column_block(short_taps.shape[0]),
        pl.BlockSpec((WIDTH, filters.shape[1]), lambda i, *_: (i, 0)),
        column_block(1),
        whole(tables[0].shape),
        whole(tables[1].shape),
    ]


def gate_late(queries, keys_in, values_in, short_taps, filters, skip_gain, tables):
    rows, channels = queries.shape
    out_rows = rows - EARLY * BLK
    return pl.pallas_call(
        functools.partial(late_kernel, EARLY),
        grid=(channels // WIDTH,),
        out_shape=jax.ShapeDtypeStruct((out_rows, channels), jnp.bfloat16),
        in_specs=[column_block(rows)] * 3 + parameter_specs(short_taps, filters, tables),
        out_specs=column_block(out_rows),
        scratch_shapes=[pltpu.VMEM((out_rows + BLK, WIDTH), jnp.bfloat16)],
        compiler_params=pltpu.CompilerParams(vmem_limit_bytes=VMEM_LIMIT),
        cost_estimate=pl.CostEstimate(flops=4 * 10**9, bytes_accessed=3 * 10**6, transcendentals=0),
        name="gate_late",
    )(*map(stay, (queries, keys_in, values_in, short_taps, filters, skip_gain, *tables)))


def gate_early(place, queries, keys_in, values_in, halo, late, short_taps, filters, skip_gain, tables):
    rows, channels = queries.shape
    half = jax.ShapeDtypeStruct((rows // 2, channels), jnp.bfloat16)
    return pl.pallas_call(
        early_kernel,
        grid_spec=pltpu.PrefetchScalarGridSpec(
            num_scalar_prefetch=2,
            grid=(channels // WIDTH,),
            in_specs=[column_block(EARLY * BLK)] * 3
            + [column_block(halo.shape[0]), column_block(late.shape[0])]
            + parameter_specs(short_taps, filters, tables),
            out_specs=[column_block(rows // 2)] * 2,
            scratch_shapes=[
                pltpu.VMEM(((EARLY + 1) * BLK, WIDTH), jnp.bfloat16),
                pltpu.VMEM((rows, WIDTH), jnp.bfloat16),
            ],
        ),
        out_shape=[half, half],
        compiler_params=pltpu.CompilerParams(vmem_limit_bytes=VMEM_LIMIT),
        cost_estimate=pl.CostEstimate(flops=2 * 10**9, bytes_accessed=3 * 10**6, transcendentals=0),
        name="gate_early",
    )(
        place,
        jnp.asarray(row_order()),
        *map(stay, (queries, keys_in, values_in)),
        halo,
        late,
        *map(stay, (short_taps, filters, skip_gain, *tables)),
    )


def project_kernel(first, count, tile, pieces, a_ref, b_ref, wa_ref, wb_ref, *out_refs):
    depth = wa_ref.shape[0]

    def step(wa, wb, *outs):
        acc = jnp.dot(a_ref[...], wa[...], preferred_element_type=jnp.float32)
        acc = acc + jnp.dot(b_ref[...], wb[...], preferred_element_type=jnp.float32)
        acc = acc.astype(jnp.bfloat16)
        for ref, spans in zip(outs, pieces):
            at = 0
            for start, stop in spans:
                ref[at : at + stop - start] = acc[start:stop]
                at += stop - start

    rhs = pl.BlockSpec((depth, tile), lambda j: (0, j))
    pltpu.emit_pipeline(
        step,
        grid=(count // tile,),
        in_specs=[rhs, rhs],
        out_specs=[pl.BlockSpec((ref.shape[0], tile), lambda j: (0, j)) for ref in out_refs],
    )(wa_ref.at[:, pl.ds(first, count)], wb_ref.at[:, pl.ds(first, count)], *out_refs)


def project(mine, theirs, weight, weight_pair, first, count, tile, pieces):
    rows, depth = mine.shape
    sizes = [sum(stop - start for start, stop in spans) for spans in pieces]
    anywhere = pl.BlockSpec(memory_space=pl.ANY)
    return pl.pallas_call(
        functools.partial(project_kernel, first, count, tile, pieces),
        out_shape=[jax.ShapeDtypeStruct((n, count), jnp.bfloat16) for n in sizes],
        in_specs=[pl.BlockSpec(memory_space=pltpu.VMEM)] * 2 + [pl.BlockSpec(memory_space=pltpu.HBM)] * 2,
        out_specs=[anywhere] * len(sizes),
        compiler_params=pltpu.CompilerParams(vmem_limit_bytes=VMEM_LIMIT),
        cost_estimate=pl.CostEstimate(
            flops=4 * rows * depth * count, bytes_accessed=2 * (2 * depth + rows) * count, transcendentals=0
        ),
        name="project",
    )(mine, theirs, stay(weight), stay(weight_pair))


def moved(dy=0, dx=0, dc=0):
    pairs = []
    for y in range(N_Y):
        for x in range(N_X):
            for c in range(N_C):
                source = (y * N_X + x) * N_C + c
                target = (((y + dy) % N_Y) * N_X + (x + dx) % N_X) * N_C + (c + dc) % N_C
                pairs.append((source, target))
    return pairs


def send(array, **step):
    return lax.ppermute(array, "tp", moved(**step))


def add(*arrays):
    total = arrays[0].astype(jnp.float32)
    for array in arrays[1:]:
        total = total + array.astype(jnp.float32)
    return total


def reduce_y(first, second, hold=None):
    far_second = send(second[2], dy=1)
    far_first = send(first[2], dy=-1)
    up_first = send(first[1], dy=1)
    down_second = send(second[3], dy=-1)
    if hold is not None:
        far_second, far_first, _ = lax.optimization_barrier((far_second, far_first, hold))
    up_second = send(add(second[1], far_second).astype(jnp.bfloat16), dy=1)
    down_first = send(add(first[3], far_first).astype(jnp.bfloat16), dy=-1)
    return add(first[0], up_first, down_first), add(second[0], down_second, up_second)


X_FIRST = 1792


def body(queries, keys_in, values_in, short_taps, filters, skip_gain, out_weight, residual):
    rows = queries.shape[0]
    width = out_weight.shape[1]
    peers = lax.axis_size("ctx")
    piece = rows // (N_Y * N_X * N_C)
    weight_pair = send(out_weight, dc=1)
    rim = make_rim(queries, keys_in, values_in, short_taps)
    halo = lax.ppermute(rim, "ctx", [(i, i + 1) for i in range(peers - 1)])
    parameters = (short_taps, filters, skip_gain[None, :], transform_tables(filters.shape[1]))
    late = gate_late(queries, keys_in, values_in, *parameters)
    place = lax.axis_index("tp").astype(jnp.int32)[None]
    keep, give = gate_early(place, queries, keys_in, values_in, halo, late, *parameters)
    theirs = send(give, dc=1)

    half = rows // (2 * N_C)
    by_x = (((0, half),), ((half, 2 * half),))
    by_y = tuple(((s * piece, (s + 1) * piece), (half + s * piece, half + (s + 1) * piece)) for s in range(N_Y))
    y_first = width // 2 - X_FIRST

    def multiply(after, *where):
        left = lax.optimization_barrier((keep, after))[0]
        return project(left, theirs, out_weight, weight_pair, *where)

    a0_keep, a0_give = multiply(place, 0, X_FIRST, X_FIRST // 2, by_x)
    a0_got = send(a0_give, dx=1)
    b0 = multiply(a0_keep, 2 * X_FIRST, y_first, y_first // 2, by_y)
    b1 = multiply(b0[0], 2 * X_FIRST + y_first, y_first, y_first // 2, by_y)
    a1_keep, a1_give = multiply(b1[0], X_FIRST, X_FIRST, X_FIRST // 2, by_x)
    a1_got = send(lax.optimization_barrier((a1_give, a0_got))[0], dx=1)
    b0_sum, b1_sum = reduce_y(b0, b1, a0_got)
    b0_give, b1_give = b0_sum[piece:].astype(jnp.bfloat16), b1_sum[piece:].astype(jnp.bfloat16)
    b0_sum, b1_sum = b0_sum[:piece], b1_sum[:piece]
    a0_got, a1_got, b0_give, b1_give = lax.optimization_barrier((a0_got, a1_got, b0_give, b1_give))

    b0_got = send(b0_give, dx=1)
    b1_give = lax.optimization_barrier((b1_give, b0_got))[0]
    b1_got = send(b1_give, dx=1)

    def sections(keep_part, got):
        total = add(keep_part, got)
        return [total[:piece]] + [total[s * piece : (s + 1) * piece].astype(jnp.bfloat16) for s in range(1, N_Y)]

    a0_sum, a1_sum = reduce_y(sections(a0_keep, a0_got), sections(a1_keep, a1_got), b0_got)
    summed = jnp.concatenate([a0_sum, a1_sum, add(b0_sum, b0_got), add(b1_sum, b1_got)], axis=1)
    return (residual.astype(jnp.float32) + summed).astype(jnp.bfloat16)


def solution(mesh):
    in_specs = (
        P("ctx", "tp"),
        P("ctx", "tp"),
        P("ctx", "tp"),
        P(None, "tp"),
        P("tp", None),
        P("tp"),
        P("tp", None),
        P(("ctx", "tp"), None),
    )
    out_specs = P(("ctx", "tp"), None)
    return jax.shard_map(body, mesh=mesh, in_specs=in_specs, out_specs=out_specs, check_vma=False)
```

```python
import math
import functools
import numpy as np
import jax
import jax.numpy as jnp
from jax import lax
from jax.experimental import pallas as pl
from jax.experimental.pallas import tpu as pltpu
from jax.sharding import PartitionSpec as P

BLK = 128
N_Y, N_X, N_C = 4, 2, 2


def split_bf16(matrix):
    high = matrix.astype(jnp.bfloat16)
    low = (matrix - high.astype(np.float64)).astype(jnp.bfloat16)
    return high, low


def transform_tables(taps):
    span = 2 * taps
    freq = np.arange(taps)[:, None] + 0.5
    time = np.arange(span)[None, :]
    angle = 2.0 * np.pi * freq * time / span
    forward = np.concatenate([np.cos(angle), -np.sin(angle)], axis=0)
    inverse = (2.0 / span) * forward.T[taps:]
    f_high, f_low = split_bf16(forward)
    g_high, g_low = split_bf16(inverse)
    return np.concatenate([f_high, f_low], axis=0), np.concatenate([g_high, g_low], axis=0)


def short_filter(wide, taps):
    rows = wide.shape[0] - 16
    total = taps[0:1] * wide[16 : 16 + rows]
    for j in range(1, taps.shape[0]):
        total = total + taps[j : j + 1] * wide[16 - j : 16 - j + rows]
    return total


def spectrum(f_ref, filt_ref):
    spec = lax.dot_general(
        f_ref[:, :BLK], filt_ref[...], (((1,), (1,)), ((), ())), preferred_element_type=jnp.float32
    )
    spec = spec[: 2 * BLK] + spec[2 * BLK :]
    return spec[:BLK], spec[BLK:]


def long_filter(span, h_re, h_im, f_ref, g_ref):
    x = jnp.dot(f_ref[...], span, preferred_element_type=jnp.float32)
    x = x[: 2 * BLK] + x[2 * BLK :]
    x_re, x_im = x[:BLK], x[BLK:]
    y = jnp.concatenate([x_re * h_re - x_im * h_im, x_re * h_im + x_im * h_re], axis=0)
    y_high = y.astype(jnp.bfloat16)
    y_low = (y - y_high.astype(jnp.float32)).astype(jnp.bfloat16)
    z = jnp.dot(g_ref[...], y_high, preferred_element_type=jnp.float32)
    return z[:BLK] + z[BLK:] + jnp.dot(g_ref[:BLK], y_low, preferred_element_type=jnp.float32)


def window(ref, b):
    return ref[b * BLK - 16 : (b + 1) * BLK].astype(jnp.float32)


def rim_kernel(q_ref, k_ref, v_ref, taps_ref, out_ref):
    taps = taps_ref[...].astype(jnp.float32)
    tail = BLK + 16
    at = k_ref.shape[0] - tail
    k_win, v_win = k_ref[at:].astype(jnp.float32), v_ref[at:].astype(jnp.float32)
    out_ref[:BLK] = (short_filter(k_win, taps) * short_filter(v_win, taps)).astype(jnp.bfloat16)
    q_end = pltpu.roll(q_ref[...].astype(jnp.float32), 2, 0)
    k_end = pltpu.roll(k_win[BLK:], 4, 0)
    v_end = pltpu.roll(v_win[BLK:], 6, 0)
    row = lax.broadcasted_iota(jnp.int32, q_end.shape, 0)
    packed = jnp.where(row < 2, q_end, jnp.where(row < 4, k_end, v_end))
    out_ref[BLK:] = packed.astype(jnp.bfloat16)


def late_kernel(first, q_ref, k_ref, v_ref, taps_ref, filt_ref, skip_ref, f_ref, g_ref, out_ref, prod_ref):
    blocks = q_ref.shape[0] // BLK
    taps = taps_ref[...].astype(jnp.float32)
    skip = skip_ref[...]
    h_re, h_im = spectrum(f_ref, filt_ref)
    for b in range(first - 1, blocks):
        at = (b - first + 1) * BLK
        prod = short_filter(window(k_ref, b), taps) * short_filter(window(v_ref, b), taps)
        prod = prod.astype(jnp.bfloat16)
        prod_ref[at : at + BLK] = prod
        if b >= first:
            filtered = long_filter(prod_ref[at - BLK : at + BLK], h_re, h_im, f_ref, g_ref)
            gated = short_filter(window(q_ref, b), taps) * (filtered + skip * prod.astype(jnp.float32))
            out_ref[at - BLK : at] = gated.astype(jnp.bfloat16)


def early_kernel(
    place_ref, order_ref, q_ref, k_ref, v_ref, halo_ref, late_ref, taps_ref, filt_ref, skip_ref, f_ref, g_ref,
    keep_ref, give_ref, prod_ref, gated_ref,
):
    blocks = q_ref.shape[0] // BLK
    taps = taps_ref[...].astype(jnp.float32)
    skip = skip_ref[...]
    rim = halo_ref[BLK:].astype(jnp.float32)

    def rows_of(ref, b, turn):
        if b == 0:
            return jnp.concatenate([pltpu.roll(rim, turn, 0), ref[:BLK].astype(jnp.float32)], axis=0)
        return window(ref, b)

    h_re, h_im = spectrum(f_ref, filt_ref)
    prod_ref[:BLK] = halo_ref[:BLK]
    for b in range(blocks):
        prod = short_filter(rows_of(k_ref, b, 12), taps) * short_filter(rows_of(v_ref, b, 10), taps)
        prod = prod.astype(jnp.bfloat16)
        prod_ref[(b + 1) * BLK : (b + 2) * BLK] = prod
        filtered = long_filter(prod_ref[b * BLK : (b + 2) * BLK], h_re, h_im, f_ref, g_ref)
        gated = short_filter(rows_of(q_ref, b, 14), taps) * (filtered + skip * prod.astype(jnp.float32))
        gated_ref[b * BLK : (b + 1) * BLK] = gated.astype(jnp.bfloat16)
    gated_ref[blocks * BLK :] = late_ref[...]

    slots = N_Y * N_X
    piece = keep_ref.shape[0] // slots
    for slot in range(slots):
        for which, ref in ((0, keep_ref), (1, give_ref)):
            group = order_ref[(place_ref[0] * 2 + which) * slots + slot]
            start = pl.multiple_of(group * piece, 16)
            ref[slot * piece : (slot + 1) * piece] = gated_ref[pl.ds(start, piece)]


def row_order():
    table = []
    for y in range(N_Y):
        for x in range(N_X):
            for c in range(N_C):
                for dc in range(N_C):
                    for dx in range(N_X):
                        for dy in range(N_Y):
                            table.append((((y + dy) % N_Y) * N_X + (x + dx) % N_X) * N_C + (c + dc) % N_C)
    return np.array(table, np.int32)


VMEM_LIMIT = 24 * 1024 * 1024
EARLY = 2
WIDTH = 256


def stay(array):
    return pltpu.with_memory_space_constraint(array, pltpu.HBM)


def column_block(rows, index=0):
    return pl.BlockSpec((rows, WIDTH), lambda i, *_: (index, i))


def whole(shape):
    return pl.BlockSpec(shape, lambda i, *_: (0, 0))


def make_rim(queries, keys_in, values_in, short_taps):
    rows, channels = queries.shape
    part = rows // 4
    return pl.pallas_call(
        rim_kernel,
        grid=(channels // WIDTH,),
        out_shape=jax.ShapeDtypeStruct((BLK + 16, channels), jnp.bfloat16),
        in_specs=[
            column_block(16, rows // 16 - 1),
            column_block(part, rows // part - 1),
            column_block(part, rows // part - 1),
            column_block(short_taps.shape[0]),
        ],
        out_specs=column_block(BLK + 16),
        compiler_params=pltpu.CompilerParams(vmem_limit_bytes=VMEM_LIMIT),
        cost_estimate=pl.CostEstimate(flops=10**9, bytes_accessed=10**6, transcendentals=0),
        name="rim",
    )(stay(queries), stay(keys_in), stay(values_in), stay(short_taps))


def parameter_specs(short_taps, filters, tables):
    return [
        column_block(short_taps.shape[0]),
        pl.BlockSpec((WIDTH, filters.shape[1]), lambda i, *_: (i, 0)),
        column_block(1),
        whole(tables[0].shape),
        whole(tables[1].shape),
    ]


def gate_late(queries, keys_in, values_in, short_taps, filters, skip_gain, tables):
    rows, channels = queries.shape
    out_rows = rows - EARLY * BLK
    return pl.pallas_call(
        functools.partial(late_kernel, EARLY),
        grid=(channels // WIDTH,),
        out_shape=jax.ShapeDtypeStruct((out_rows, channels), jnp.bfloat16),
        in_specs=[column_block(rows)] * 3 + parameter_specs(short_taps, filters, tables),
        out_specs=column_block(out_rows),
        scratch_shapes=[pltpu.VMEM((out_rows + BLK, WIDTH), jnp.bfloat16)],
        compiler_params=pltpu.CompilerParams(vmem_limit_bytes=VMEM_LIMIT),
        cost_estimate=pl.CostEstimate(flops=4 * 10**9, bytes_accessed=3 * 10**6, transcendentals=0),
        name="gate_late",
    )(*map(stay, (queries, keys_in, values_in, short_taps, filters, skip_gain, *tables)))


def gate_early(place, queries, keys_in, values_in, halo, late, short_taps, filters, skip_gain, tables):
    rows, channels = queries.shape
    half = jax.ShapeDtypeStruct((rows // 2, channels), jnp.bfloat16)
    return pl.pallas_call(
        early_kernel,
        grid_spec=pltpu.PrefetchScalarGridSpec(
            num_scalar_prefetch=2,
            grid=(channels // WIDTH,),
            in_specs=[column_block(EARLY * BLK)] * 3
            + [column_block(halo.shape[0]), column_block(late.shape[0])]
            + parameter_specs(short_taps, filters, tables),
            out_specs=[column_block(rows // 2)] * 2,
            scratch_shapes=[
                pltpu.VMEM(((EARLY + 1) * BLK, WIDTH), jnp.bfloat16),
                pltpu.VMEM((rows, WIDTH), jnp.bfloat16),
            ],
        ),
        out_shape=[half, half],
        compiler_params=pltpu.CompilerParams(vmem_limit_bytes=VMEM_LIMIT),
        cost_estimate=pl.CostEstimate(flops=2 * 10**9, bytes_accessed=3 * 10**6, transcendentals=0),
        name="gate_early",
    )(
        place,
        jnp.asarray(row_order()),
        *map(stay, (queries, keys_in, values_in)),
        halo,
        late,
        *map(stay, (short_taps, filters, skip_gain, *tables)),
    )


def project_kernel(first, count, tile, pieces, a_ref, b_ref, wa_ref, wb_ref, *out_refs):
    depth = wa_ref.shape[0]

    def step(wa, wb, *outs):
        acc = jnp.dot(a_ref[...], wa[...], preferred_element_type=jnp.float32)
        acc = acc + jnp.dot(b_ref[...], wb[...], preferred_element_type=jnp.float32)
        acc = acc.astype(jnp.bfloat16)
        for ref, spans in zip(outs, pieces):
            at = 0
            for start, stop in spans:
                ref[at : at + stop - start] = acc[start:stop]
                at += stop - start

    rhs = pl.BlockSpec((depth, tile), lambda j: (0, j))
    pltpu.emit_pipeline(
        step,
        grid=(count // tile,),
        in_specs=[rhs, rhs],
        out_specs=[pl.BlockSpec((ref.shape[0], tile), lambda j: (0, j)) for ref in out_refs],
    )(wa_ref.at[:, pl.ds(first, count)], wb_ref.at[:, pl.ds(first, count)], *out_refs)


def project(mine, theirs, weight, weight_pair, first, count, tile, pieces):
    rows, depth = mine.shape
    sizes = [sum(stop - start for start, stop in spans) for spans in pieces]
    anywhere = pl.BlockSpec(memory_space=pl.ANY)
    return pl.pallas_call(
        functools.partial(project_kernel, first, count, tile, pieces),
        out_shape=[jax.ShapeDtypeStruct((n, count), jnp.bfloat16) for n in sizes],
        in_specs=[pl.BlockSpec(memory_space=pltpu.VMEM)] * 2 + [pl.BlockSpec(memory_space=pltpu.HBM)] * 2,
        out_specs=[anywhere] * len(sizes),
        compiler_params=pltpu.CompilerParams(vmem_limit_bytes=VMEM_LIMIT),
        cost_estimate=pl.CostEstimate(
            flops=4 * rows * depth * count, bytes_accessed=2 * (2 * depth + rows) * count, transcendentals=0
        ),
        name="project",
    )(mine, theirs, stay(weight), stay(weight_pair))


def moved(dy=0, dx=0, dc=0):
    pairs = []
    for y in range(N_Y):
        for x in range(N_X):
            for c in range(N_C):
                source = (y * N_X + x) * N_C + c
                target = (((y + dy) % N_Y) * N_X + (x + dx) % N_X) * N_C + (c + dc) % N_C
                pairs.append((source, target))
    return pairs


def send(array, **step):
    return lax.ppermute(array, "tp", moved(**step))


def add(*arrays):
    total = arrays[0].astype(jnp.float32)
    for array in arrays[1:]:
        total = total + array.astype(jnp.float32)
    return total


X_FIRST = (2560, 1536)


def body(queries, keys_in, values_in, short_taps, filters, skip_gain, out_weight, residual):
    rows = queries.shape[0]
    width = out_weight.shape[1]
    peers = lax.axis_size("ctx")
    piece = rows // (N_Y * N_X * N_C)
    weight_pair = send(out_weight, dc=1)
    rim = make_rim(queries, keys_in, values_in, short_taps)
    halo = lax.ppermute(rim, "ctx", [(i, i + 1) for i in range(peers - 1)])
    parameters = (short_taps, filters, skip_gain[None, :], transform_tables(filters.shape[1]))
    late = gate_late(queries, keys_in, values_in, *parameters)
    place = lax.axis_index("tp").astype(jnp.int32)[None]
    keep, give = gate_early(place, queries, keys_in, values_in, halo, late, *parameters)
    theirs = send(give, dc=1)

    half = rows // (2 * N_C)
    by_x = (((0, half),), ((half, 2 * half),))
    by_y = tuple(((s * piece, (s + 1) * piece), (half + s * piece, half + (s + 1) * piece)) for s in range(N_Y))
    y_first = (width - sum(X_FIRST)) // 2

    def multiply(after, first, count, pieces):
        left = lax.optimization_barrier((keep, after))[0]
        return project(left, theirs, out_weight, weight_pair, first, count, count // 2, pieces)

    def narrow(array):
        return array.astype(jnp.bfloat16)

    a0_keep, a0_give = multiply(place, 0, X_FIRST[0], by_x)
    a0_got = send(a0_give, dx=1)
    b0 = multiply(a0_keep, sum(X_FIRST), y_first, by_y)
    b1 = multiply(b0[0], sum(X_FIRST) + y_first, y_first, by_y)
    a1_keep, a1_give = multiply(b1[0], X_FIRST[0], X_FIRST[1], by_x)

    b1_far = send(b1[2], dy=1)
    b0_far = send(b0[2], dy=-1)
    b0_up = send(b0[1], dy=1)
    b1_down = send(b1[3], dy=-1)
    a1_got = send(lax.optimization_barrier((a1_give, a0_got))[0], dx=1)

    b0_far, b1_far, a0_got = lax.optimization_barrier((b0_far, b1_far, a0_got))
    b1_up = send(narrow(add(b1[1], b1_far)), dy=1)
    b0_down = send(narrow(add(b0[3], b0_far)), dy=-1)

    a0, a1 = add(a0_keep, a0_got), add(a1_keep, a1_got)
    edge = sum(X_FIRST) // 2
    low = [a0[s * piece : (s + 1) * piece, :edge] for s in range(N_Y)]
    high = [
        jnp.concatenate([a0[s * piece : (s + 1) * piece, edge:], a1[s * piece : (s + 1) * piece]], axis=1)
        for s in range(N_Y)
    ]
    low_send, high_send = [narrow(part) for part in low], [narrow(part) for part in high]
    low_send, high_send = lax.optimization_barrier((low_send, high_send))
    low_far = send(low_send[2], dy=-1)
    high_far = send(high_send[2], dy=1)

    b0_sum, b1_sum = add(b0[0], b0_up, b0_down), add(b1[0], b1_up, b1_down)
    b0_give, b1_give = narrow(b0_sum[piece:]), narrow(b1_sum[piece:])
    b0_give, b1_give, low_send[1], high_send[3] = lax.optimization_barrier((b0_give, b1_give, low_send[1], high_send[3]))
    b0_got = send(b0_give, dx=1)
    low_up = send(low_send[1], dy=1)
    high_down = send(high_send[3], dy=-1)

    b0_got, b1_give = lax.optimization_barrier((b0_got, b1_give))
    low_down = send(narrow(add(low[3], low_far)), dy=-1)
    high_up = send(narrow(add(high[1], high_far)), dy=1)
    b1_got = send(b1_give, dx=1)

    summed = jnp.concatenate(
        [
            add(low[0], low_up, low_down),
            add(high[0], high_down, high_up),
            add(b0_sum[:piece], b0_got),
            add(b1_sum[:piece], b1_got),
        ],
        axis=1,
    )
    return narrow(residual.astype(jnp.float32) + summed)


def solution(mesh):
    in_specs = (
        P("ctx", "tp"),
        P("ctx", "tp"),
        P("ctx", "tp"),
        P(None, "tp"),
        P("tp", None),
        P("tp"),
        P("tp", None),
        P(("ctx", "tp"), None),
    )
    out_specs = P(("ctx", "tp"), None)
    return jax.shard_map(body, mesh=mesh, in_specs=in_specs, out_specs=out_specs, check_vma=False)
```

```python
import math
import functools
import numpy as np
import jax
import jax.numpy as jnp
from jax import lax
from jax.experimental import pallas as pl
from jax.experimental.pallas import tpu as pltpu
from jax.sharding import PartitionSpec as P

BLK = 128
N_Y, N_X, N_C = 4, 2, 2


def split_bf16(matrix):
    high = matrix.astype(jnp.bfloat16)
    low = (matrix - high.astype(np.float64)).astype(jnp.bfloat16)
    return high, low


def transform_tables(taps):
    span = 2 * taps
    freq = np.arange(taps)[:, None] + 0.5
    time = np.arange(span)[None, :]
    angle = 2.0 * np.pi * freq * time / span
    forward = np.concatenate([np.cos(angle), -np.sin(angle)], axis=0)
    inverse = (2.0 / span) * forward.T[taps:]
    f_high, f_low = split_bf16(forward)
    g_high, g_low = split_bf16(inverse)
    return np.concatenate([f_high, f_low], axis=0), np.concatenate([g_high, g_low], axis=0)


def short_filter(wide, taps):
    rows = wide.shape[0] - 16
    total = taps[0:1] * wide[16 : 16 + rows]
    for j in range(1, taps.shape[0]):
        total = total + taps[j : j + 1] * wide[16 - j : 16 - j + rows]
    return total


def spectrum(f_ref, filt_ref):
    spec = lax.dot_general(
        f_ref[:, :BLK], filt_ref[...], (((1,), (1,)), ((), ())), preferred_element_type=jnp.float32
    )
    spec = spec[: 2 * BLK] + spec[2 * BLK :]
    return spec[:BLK], spec[BLK:]


def long_filter(span, h_re, h_im, f_ref, g_ref):
    x = jnp.dot(f_ref[...], span, preferred_element_type=jnp.float32)
    x = x[: 2 * BLK] + x[2 * BLK :]
    x_re, x_im = x[:BLK], x[BLK:]
    y = jnp.concatenate([x_re * h_re - x_im * h_im, x_re * h_im + x_im * h_re], axis=0)
    y_high = y.astype(jnp.bfloat16)
    y_low = (y - y_high.astype(jnp.float32)).astype(jnp.bfloat16)
    z = jnp.dot(g_ref[...], y_high, preferred_element_type=jnp.float32)
    return z[:BLK] + z[BLK:] + jnp.dot(g_ref[:BLK], y_low, preferred_element_type=jnp.float32)


def window(ref, b):
    return ref[b * BLK - 16 : (b + 1) * BLK].astype(jnp.float32)


def rim_kernel(q_ref, k_ref, v_ref, taps_ref, out_ref):
    taps = taps_ref[...].astype(jnp.float32)
    tail = BLK + 16
    at = k_ref.shape[0] - tail
    k_win, v_win = k_ref[at:].astype(jnp.float32), v_ref[at:].astype(jnp.float32)
    out_ref[:BLK] = (short_filter(k_win, taps) * short_filter(v_win, taps)).astype(jnp.bfloat16)
    q_end = pltpu.roll(q_ref[...].astype(jnp.float32), 2, 0)
    k_end = pltpu.roll(k_win[BLK:], 4, 0)
    v_end = pltpu.roll(v_win[BLK:], 6, 0)
    row = lax.broadcasted_iota(jnp.int32, q_end.shape, 0)
    packed = jnp.where(row < 2, q_end, jnp.where(row < 4, k_end, v_end))
    out_ref[BLK:] = packed.astype(jnp.bfloat16)


def late_kernel(first, q_ref, k_ref, v_ref, taps_ref, filt_ref, skip_ref, f_ref, g_ref, out_ref, prod_ref):
    blocks = q_ref.shape[0] // BLK
    taps = taps_ref[...].astype(jnp.float32)
    skip = skip_ref[...]
    h_re, h_im = spectrum(f_ref, filt_ref)
    for b in range(first - 1, blocks):
        at = (b - first + 1) * BLK
        prod = short_filter(window(k_ref, b), taps) * short_filter(window(v_ref, b), taps)
        prod = prod.astype(jnp.bfloat16)
        prod_ref[at : at + BLK] = prod
        if b >= first:
            filtered = long_filter(prod_ref[at - BLK : at + BLK], h_re, h_im, f_ref, g_ref)
            gated = short_filter(window(q_ref, b), taps) * (filtered + skip * prod.astype(jnp.float32))
            out_ref[at - BLK : at] = gated.astype(jnp.bfloat16)


def early_kernel(
    place_ref, order_ref, q_ref, k_ref, v_ref, halo_ref, late_ref, taps_ref, filt_ref, skip_ref, f_ref, g_ref,
    keep_ref, give_ref, prod_ref, gated_ref,
):
    blocks = q_ref.shape[0] // BLK
    taps = taps_ref[...].astype(jnp.float32)
    skip = skip_ref[...]
    rim = halo_ref[BLK:].astype(jnp.float32)

    def rows_of(ref, b, turn):
        if b == 0:
            return jnp.concatenate([pltpu.roll(rim, turn, 0), ref[:BLK].astype(jnp.float32)], axis=0)
        return window(ref, b)

    h_re, h_im = spectrum(f_ref, filt_ref)
    prod_ref[:BLK] = halo_ref[:BLK]
    for b in range(blocks):
        prod = short_filter(rows_of(k_ref, b, 12), taps) * short_filter(rows_of(v_ref, b, 10), taps)
        prod = prod.astype(jnp.bfloat16)
        prod_ref[(b + 1) * BLK : (b + 2) * BLK] = prod
        filtered = long_filter(prod_ref[b * BLK : (b + 2) * BLK], h_re, h_im, f_ref, g_ref)
        gated = short_filter(rows_of(q_ref, b, 14), taps) * (filtered + skip * prod.astype(jnp.float32))
        gated_ref[b * BLK : (b + 1) * BLK] = gated.astype(jnp.bfloat16)
    gated_ref[blocks * BLK :] = late_ref[...]

    slots = N_Y * N_X
    piece = keep_ref.shape[0] // slots
    for slot in range(slots):
        for which, ref in ((0, keep_ref), (1, give_ref)):
            group = order_ref[(place_ref[0] * 2 + which) * slots + slot]
            start = pl.multiple_of(group * piece, 16)
            ref[slot * piece : (slot + 1) * piece] = gated_ref[pl.ds(start, piece)]


def row_order():
    table = []
    for y in range(N_Y):
        for x in range(N_X):
            for c in range(N_C):
                for dc in range(N_C):
                    for dx in range(N_X):
                        for dy in range(N_Y):
                            table.append((((y + dy) % N_Y) * N_X + (x + dx) % N_X) * N_C + (c + dc) % N_C)
    return np.array(table, np.int32)


VMEM_LIMIT = 24 * 1024 * 1024
EARLY = 2
WIDTH = 256


def stay(array):
    return pltpu.with_memory_space_constraint(array, pltpu.HBM)


def column_block(rows, index=0):
    return pl.BlockSpec((rows, WIDTH), lambda i, *_: (index, i))


def whole(shape):
    return pl.BlockSpec(shape, lambda i, *_: (0, 0))


def make_rim(queries, keys_in, values_in, short_taps):
    rows, channels = queries.shape
    part = rows // 4
    return pl.pallas_call(
        rim_kernel,
        grid=(channels // WIDTH,),
        out_shape=jax.ShapeDtypeStruct((BLK + 16, channels), jnp.bfloat16),
        in_specs=[
            column_block(16, rows // 16 - 1),
            column_block(part, rows // part - 1),
            column_block(part, rows // part - 1),
            column_block(short_taps.shape[0]),
        ],
        out_specs=column_block(BLK + 16),
        compiler_params=pltpu.CompilerParams(vmem_limit_bytes=VMEM_LIMIT),
        cost_estimate=pl.CostEstimate(flops=10**9, bytes_accessed=10**6, transcendentals=0),
        name="rim",
    )(stay(queries), stay(keys_in), stay(values_in), stay(short_taps))


def parameter_specs(short_taps, filters, tables):
    return [
        column_block(short_taps.shape[0]),
        pl.BlockSpec((WIDTH, filters.shape[1]), lambda i, *_: (i, 0)),
        column_block(1),
        whole(tables[0].shape),
        whole(tables[1].shape),
    ]


def gate_late(queries, keys_in, values_in, short_taps, filters, skip_gain, tables):
    rows, channels = queries.shape
    out_rows = rows - EARLY * BLK
    return pl.pallas_call(
        functools.partial(late_kernel, EARLY),
        grid=(channels // WIDTH,),
        out_shape=jax.ShapeDtypeStruct((out_rows, channels), jnp.bfloat16),
        in_specs=[column_block(rows)] * 3 + parameter_specs(short_taps, filters, tables),
        out_specs=column_block(out_rows),
        scratch_shapes=[pltpu.VMEM((out_rows + BLK, WIDTH), jnp.bfloat16)],
        compiler_params=pltpu.CompilerParams(vmem_limit_bytes=VMEM_LIMIT),
        cost_estimate=pl.CostEstimate(flops=4 * 10**9, bytes_accessed=3 * 10**6, transcendentals=0),
        name="gate_late",
    )(*map(stay, (queries, keys_in, values_in, short_taps, filters, skip_gain, *tables)))


def gate_early(place, queries, keys_in, values_in, halo, late, short_taps, filters, skip_gain, tables):
    rows, channels = queries.shape
    half = jax.ShapeDtypeStruct((rows // 2, channels), jnp.bfloat16)
    return pl.pallas_call(
        early_kernel,
        grid_spec=pltpu.PrefetchScalarGridSpec(
            num_scalar_prefetch=2,
            grid=(channels // WIDTH,),
            in_specs=[column_block(EARLY * BLK)] * 3
            + [column_block(halo.shape[0]), column_block(late.shape[0])]
            + parameter_specs(short_taps, filters, tables),
            out_specs=[column_block(rows // 2)] * 2,
            scratch_shapes=[
                pltpu.VMEM(((EARLY + 1) * BLK, WIDTH), jnp.bfloat16),
                pltpu.VMEM((rows, WIDTH), jnp.bfloat16),
            ],
        ),
        out_shape=[half, half],
        compiler_params=pltpu.CompilerParams(vmem_limit_bytes=VMEM_LIMIT),
        cost_estimate=pl.CostEstimate(flops=2 * 10**9, bytes_accessed=3 * 10**6, transcendentals=0),
        name="gate_early",
    )(
        place,
        jnp.asarray(row_order()),
        *map(stay, (queries, keys_in, values_in)),
        halo,
        late,
        *map(stay, (short_taps, filters, skip_gain, *tables)),
    )


def scatter_rows(acc, refs, pieces):
    acc = acc.astype(jnp.bfloat16)
    for ref, spans in zip(refs, pieces):
        at = 0
        for start, stop in spans:
            ref[at : at + stop - start] = acc[start:stop]
            at += stop - start


def both_products(a_ref, b_ref, wa_ref, wb_ref):
    acc = jnp.dot(a_ref[...], wa_ref[...], preferred_element_type=jnp.float32)
    return acc + jnp.dot(b_ref[...], wb_ref[...], preferred_element_type=jnp.float32)


def own_kernel(a_ref, wa_ref, part_ref):
    part_ref[...] = jnp.dot(a_ref[...], wa_ref[...], preferred_element_type=jnp.float32)


def rest_kernel(pieces, b_ref, wb_ref, part_ref, *out_refs):
    acc = part_ref[...] + jnp.dot(b_ref[...], wb_ref[...], preferred_element_type=jnp.float32)
    scatter_rows(acc, out_refs, pieces)


def project_kernel(pieces, half, a_ref, b_ref, wa_ref, wb_ref, *out_refs):
    acc = both_products(a_ref, b_ref, wa_ref, wb_ref)
    if half is None:
        scatter_rows(acc, out_refs, pieces)
        return
    j = pl.program_id(0)

    @pl.when(j < half)
    def _():
        scatter_rows(acc, out_refs[: len(pieces)], pieces)

    @pl.when(j >= half)
    def _():
        scatter_rows(acc, out_refs[len(pieces) :], pieces)


def project_call(kernel, operands, specs, out_shape, out_specs, count, tile, depth, name):
    rows = operands[0].shape[0]
    return pl.pallas_call(
        kernel,
        grid=(count // tile,),
        out_shape=out_shape,
        in_specs=specs,
        out_specs=out_specs,
        compiler_params=pltpu.CompilerParams(vmem_limit_bytes=VMEM_LIMIT),
        cost_estimate=pl.CostEstimate(
            flops=2 * rows * depth * count, bytes_accessed=2 * (depth + rows) * count, transcendentals=0
        ),
        name=name,
    )(*operands)


def weight_block(depth, first, tile):
    return pl.BlockSpec((depth, tile), lambda j: (0, j + first // tile))


def row_sizes(pieces):
    return [sum(stop - start for start, stop in spans) for spans in pieces]


def project_own(mine, weight, first, count, tile):
    rows, depth = mine.shape
    return project_call(
        own_kernel,
        (mine, stay(weight)),
        [pl.BlockSpec((rows, depth), lambda j: (0, 0)), weight_block(depth, first, tile)],
        jax.ShapeDtypeStruct((rows, count), jnp.float32),
        pl.BlockSpec((rows, tile), lambda j: (0, j)),
        count,
        tile,
        depth,
        "project_own",
    )


def project_rest(theirs, weight_pair, part, first, tile, pieces):
    rows, depth = theirs.shape
    count = part.shape[1]
    return project_call(
        functools.partial(rest_kernel, pieces),
        (theirs, stay(weight_pair), part),
        [
            pl.BlockSpec((rows, depth), lambda j: (0, 0)),
            weight_block(depth, first, tile),
            pl.BlockSpec((rows, tile), lambda j: (0, j)),
        ],
        [jax.ShapeDtypeStruct((n, count), jnp.bfloat16) for n in row_sizes(pieces)],
        [pl.BlockSpec((n, tile), lambda j: (0, j)) for n in row_sizes(pieces)],
        count,
        tile,
        depth,
        "project_rest",
    )


def project(mine, theirs, weight, weight_pair, first, count, tile, pieces, halves=False):
    rows, depth = mine.shape
    lhs = pl.BlockSpec((rows, depth), lambda j: (0, 0))
    rhs = weight_block(depth, first, tile)
    sizes = row_sizes(pieces)
    if halves:
        half = count // tile // 2
        shapes = [jax.ShapeDtypeStruct((n, count // 2), jnp.bfloat16) for n in sizes] * 2
        out_specs = [pl.BlockSpec((n, tile), lambda j: (0, jnp.minimum(j, half - 1))) for n in sizes]
        out_specs += [pl.BlockSpec((n, tile), lambda j: (0, jnp.maximum(j - half, 0))) for n in sizes]
    else:
        half = None
        shapes = [jax.ShapeDtypeStruct((n, count), jnp.bfloat16) for n in sizes]
        out_specs = [pl.BlockSpec((n, tile), lambda j: (0, j)) for n in sizes]
    return project_call(
        functools.partial(project_kernel, pieces, half),
        (mine, theirs, stay(weight), stay(weight_pair)),
        [lhs, lhs, rhs, rhs],
        shapes,
        out_specs,
        count,
        tile,
        2 * depth,
        "project",
    )


def moved(dy=0, dx=0, dc=0):
    pairs = []
    for y in range(N_Y):
        for x in range(N_X):
            for c in range(N_C):
                source = (y * N_X + x) * N_C + c
                target = (((y + dy) % N_Y) * N_X + (x + dx) % N_X) * N_C + (c + dc) % N_C
                pairs.append((source, target))
    return pairs


def send(array, **step):
    return lax.ppermute(array, "tp", moved(**step))


def add(*arrays):
    total = arrays[0].astype(jnp.float32)
    for array in arrays[1:]:
        total = total + array.astype(jnp.float32)
    return total


X_FIRST = (2560, 1536)


def body(queries, keys_in, values_in, short_taps, filters, skip_gain, out_weight, residual):
    rows = queries.shape[0]
    width = out_weight.shape[1]
    peers = lax.axis_size("ctx")
    piece = rows // (N_Y * N_X * N_C)
    weight_pair = send(out_weight, dc=1)
    rim = make_rim(queries, keys_in, values_in, short_taps)
    halo = lax.ppermute(rim, "ctx", [(i, i + 1) for i in range(peers - 1)])
    parameters = (short_taps, filters, skip_gain[None, :], transform_tables(filters.shape[1]))
    late = gate_late(queries, keys_in, values_in, *parameters)
    place = lax.axis_index("tp").astype(jnp.int32)[None]
    keep, give = gate_early(place, queries, keys_in, values_in, halo, late, *parameters)
    theirs = send(give, dc=1)

    half = rows // (2 * N_C)
    by_x = (((0, half),), ((half, 2 * half),))
    by_y = tuple(((s * piece, (s + 1) * piece), (half + s * piece, half + (s + 1) * piece)) for s in range(N_Y))

    def narrow(array):
        return array.astype(jnp.bfloat16)

    edge = sum(X_FIRST)
    a0_part = project_own(keep, out_weight, 0, X_FIRST[0], X_FIRST[0] // 2)
    a0_keep, a0_give = project_rest(theirs, weight_pair, a0_part, 0, X_FIRST[0] // 2, by_x)
    a0_got = send(a0_give, dx=1)
    left = lax.optimization_barrier((keep, a0_keep))[0]
    tile = (width - edge) // 4
    b_all = project(left, theirs, out_weight, weight_pair, edge, width - edge, tile, by_y, halves=True)
    b0, b1 = b_all[:N_Y], b_all[N_Y:]
    left = lax.optimization_barrier((keep, b0[0]))[0]
    a1_keep, a1_give = project(
        left, theirs, out_weight, weight_pair, X_FIRST[0], X_FIRST[1], math.gcd(*X_FIRST), by_x
    )

    b1_far = send(b1[2], dy=1)
    b0_far = send(b0[2], dy=-1)
    b0_up = send(b0[1], dy=1)
    b1_down = send(b1[3], dy=-1)
    a1_got = send(lax.optimization_barrier((a1_give, a0_got))[0], dx=1)

    b0_far, b1_far, a0_got = lax.optimization_barrier((b0_far, b1_far, a0_got))
    b1_up = send(narrow(add(b1[1], b1_far)), dy=1)
    b0_down = send(narrow(add(b0[3], b0_far)), dy=-1)

    a0, a1 = add(a0_keep, a0_got), add(a1_keep, a1_got)
    edge = sum(X_FIRST) // 2
    low = [a0[s * piece : (s + 1) * piece, :edge] for s in range(N_Y)]
    high = [
        jnp.concatenate([a0[s * piece : (s + 1) * piece, edge:], a1[s * piece : (s + 1) * piece]], axis=1)
        for s in range(N_Y)
    ]
    low_send, high_send = [narrow(part) for part in low], [narrow(part) for part in high]
    low_send, high_send = lax.optimization_barrier((low_send, high_send))
    low_far = send(low_send[2], dy=-1)
    high_far = send(high_send[2], dy=1)

    b0_sum, b1_sum = add(b0[0], b0_up, b0_down), add(b1[0], b1_up, b1_down)
    b0_give, b1_give = narrow(b0_sum[piece:]), narrow(b1_sum[piece:])
    b0_give, b1_give, low_send[1], high_send[3] = lax.optimization_barrier((b0_give, b1_give, low_send[1], high_send[3]))
    b0_got = send(b0_give, dx=1)
    low_up = send(low_send[1], dy=1)
    high_down = send(high_send[3], dy=-1)

    low_far, high_far, b0_got, b1_give = lax.optimization_barrier((low_far, high_far, b0_got, b1_give))
    low_down = send(narrow(add(low[3], low_far)), dy=-1)
    high_up = send(narrow(add(high[1], high_far)), dy=1)
    b1_got = send(b1_give, dx=1)

    summed = jnp.concatenate(
        [
            add(low[0], low_up, low_down),
            add(high[0], high_down, high_up),
            add(b0_sum[:piece], b0_got),
            add(b1_sum[:piece], b1_got),
        ],
        axis=1,
    )
    return narrow(residual.astype(jnp.float32) + summed)


def solution(mesh):
    in_specs = (
        P("ctx", "tp"),
        P("ctx", "tp"),
        P("ctx", "tp"),
        P(None, "tp"),
        P("tp", None),
        P("tp"),
        P("tp", None),
        P(("ctx", "tp"), None),
    )
    out_specs = P(("ctx", "tp"), None)
    return jax.shard_map(body, mesh=mesh, in_specs=in_specs, out_specs=out_specs, check_vma=False)
```

```python
import math
import functools
import numpy as np
import jax
import jax.numpy as jnp
from jax import lax
from jax.experimental import pallas as pl
from jax.experimental.pallas import tpu as pltpu
from jax.sharding import PartitionSpec as P

BLK = 128
N_Y, N_X, N_C = 4, 2, 2


def split_bf16(matrix):
    high = matrix.astype(jnp.bfloat16)
    low = (matrix - high.astype(np.float64)).astype(jnp.bfloat16)
    return high, low


def transform_tables(taps):
    span = 2 * taps
    freq = np.arange(taps)[:, None] + 0.5
    time = np.arange(span)[None, :]
    angle = 2.0 * np.pi * freq * time / span
    forward = np.concatenate([np.cos(angle), -np.sin(angle)], axis=0)
    inverse = (2.0 / span) * forward.T[taps:]
    f_high, f_low = split_bf16(forward)
    g_high, g_low = split_bf16(inverse)
    return np.concatenate([f_high, f_low], axis=0), np.concatenate([g_high, g_low], axis=0)


def short_filter(wide, taps):
    rows = wide.shape[0] - 16
    total = taps[0:1] * wide[16 : 16 + rows]
    for j in range(1, taps.shape[0]):
        total = total + taps[j : j + 1] * wide[16 - j : 16 - j + rows]
    return total


def spectrum(f_ref, filt_ref):
    spec = lax.dot_general(
        f_ref[:, :BLK], filt_ref[...], (((1,), (1,)), ((), ())), preferred_element_type=jnp.float32
    )
    spec = spec[: 2 * BLK] + spec[2 * BLK :]
    return spec[:BLK], spec[BLK:]


def long_filter(span, h_re, h_im, f_ref, g_ref):
    x = jnp.dot(f_ref[...], span, preferred_element_type=jnp.float32)
    x = x[: 2 * BLK] + x[2 * BLK :]
    x_re, x_im = x[:BLK], x[BLK:]
    y = jnp.concatenate([x_re * h_re - x_im * h_im, x_re * h_im + x_im * h_re], axis=0)
    y_high = y.astype(jnp.bfloat16)
    y_low = (y - y_high.astype(jnp.float32)).astype(jnp.bfloat16)
    z = jnp.dot(g_ref[...], y_high, preferred_element_type=jnp.float32)
    return z[:BLK] + z[BLK:] + jnp.dot(g_ref[:BLK], y_low, preferred_element_type=jnp.float32)


def window(ref, b):
    return ref[b * BLK - 16 : (b + 1) * BLK].astype(jnp.float32)


def rim_kernel(q_ref, k_ref, v_ref, taps_ref, out_ref):
    taps = taps_ref[...].astype(jnp.float32)
    tail = BLK + 16
    at = k_ref.shape[0] - tail
    k_win, v_win = k_ref[at:].astype(jnp.float32), v_ref[at:].astype(jnp.float32)
    out_ref[:BLK] = (short_filter(k_win, taps) * short_filter(v_win, taps)).astype(jnp.bfloat16)
    q_end = pltpu.roll(q_ref[...].astype(jnp.float32), 2, 0)
    k_end = pltpu.roll(k_win[BLK:], 4, 0)
    v_end = pltpu.roll(v_win[BLK:], 6, 0)
    row = lax.broadcasted_iota(jnp.int32, q_end.shape, 0)
    packed = jnp.where(row < 2, q_end, jnp.where(row < 4, k_end, v_end))
    out_ref[BLK:] = packed.astype(jnp.bfloat16)


def late_kernel(first, q_ref, k_ref, v_ref, taps_ref, filt_ref, skip_ref, f_ref, g_ref, out_ref, prod_ref):
    blocks = q_ref.shape[0] // BLK
    taps = taps_ref[...].astype(jnp.float32)
    skip = skip_ref[...]
    h_re, h_im = spectrum(f_ref, filt_ref)
    for b in range(first - 1, blocks):
        at = (b - first + 1) * BLK
        prod = short_filter(window(k_ref, b), taps) * short_filter(window(v_ref, b), taps)
        prod = prod.astype(jnp.bfloat16)
        prod_ref[at : at + BLK] = prod
        if b >= first:
            filtered = long_filter(prod_ref[at - BLK : at + BLK], h_re, h_im, f_ref, g_ref)
            gated = short_filter(window(q_ref, b), taps) * (filtered + skip * prod.astype(jnp.float32))
            out_ref[at - BLK : at] = gated.astype(jnp.bfloat16)


def early_kernel(
    place_ref, order_ref, q_ref, k_ref, v_ref, halo_ref, late_ref, taps_ref, filt_ref, skip_ref, f_ref, g_ref,
    keep_ref, give_ref, prod_ref, gated_ref,
):
    blocks = q_ref.shape[0] // BLK
    taps = taps_ref[...].astype(jnp.float32)
    skip = skip_ref[...]
    rim = halo_ref[BLK:].astype(jnp.float32)

    def rows_of(ref, b, turn):
        if b == 0:
            return jnp.concatenate([pltpu.roll(rim, turn, 0), ref[:BLK].astype(jnp.float32)], axis=0)
        return window(ref, b)

    h_re, h_im = spectrum(f_ref, filt_ref)
    prod_ref[:BLK] = halo_ref[:BLK]
    for b in range(blocks):
        prod = short_filter(rows_of(k_ref, b, 12), taps) * short_filter(rows_of(v_ref, b, 10), taps)
        prod = prod.astype(jnp.bfloat16)
        prod_ref[(b + 1) * BLK : (b + 2) * BLK] = prod
        filtered = long_filter(prod_ref[b * BLK : (b + 2) * BLK], h_re, h_im, f_ref, g_ref)
        gated = short_filter(rows_of(q_ref, b, 14), taps) * (filtered + skip * prod.astype(jnp.float32))
        gated_ref[b * BLK : (b + 1) * BLK] = gated.astype(jnp.bfloat16)
    gated_ref[blocks * BLK :] = late_ref[...]

    slots = N_Y * N_X
    piece = keep_ref.shape[0] // slots
    for slot in range(slots):
        for which, ref in ((0, keep_ref), (1, give_ref)):
            group = order_ref[(place_ref[0] * 2 + which) * slots + slot]
            start = pl.multiple_of(group * piece, 16)
            ref[slot * piece : (slot + 1) * piece] = gated_ref[pl.ds(start, piece)]


def row_order():
    table = []
    for y in range(N_Y):
        for x in range(N_X):
            for c in range(N_C):
                for dc in range(N_C):
                    for dx in range(N_X):
                        for dy in range(N_Y):
                            table.append((((y + dy) % N_Y) * N_X + (x + dx) % N_X) * N_C + (c + dc) % N_C)
    return np.array(table, np.int32)


VMEM_LIMIT = 24 * 1024 * 1024
EARLY = 2
WIDTH = 256


def stay(array):
    return pltpu.with_memory_space_constraint(array, pltpu.HBM)


def column_block(rows, index=0):
    return pl.BlockSpec((rows, WIDTH), lambda i, *_: (index, i))


def whole(shape):
    return pl.BlockSpec(shape, lambda i, *_: (0, 0))


def make_rim(queries, keys_in, values_in, short_taps):
    rows, channels = queries.shape
    part = rows // 4
    return pl.pallas_call(
        rim_kernel,
        grid=(channels // WIDTH,),
        out_shape=jax.ShapeDtypeStruct((BLK + 16, channels), jnp.bfloat16),
        in_specs=[
            column_block(16, rows // 16 - 1),
            column_block(part, rows // part - 1),
            column_block(part, rows // part - 1),
            column_block(short_taps.shape[0]),
        ],
        out_specs=column_block(BLK + 16),
        compiler_params=pltpu.CompilerParams(vmem_limit_bytes=VMEM_LIMIT),
        cost_estimate=pl.CostEstimate(flops=10**9, bytes_accessed=10**6, transcendentals=0),
        name="rim",
    )(stay(queries), stay(keys_in), stay(values_in), stay(short_taps))


def parameter_specs(short_taps, filters, tables):
    return [
        column_block(short_taps.shape[0]),
        pl.BlockSpec((WIDTH, filters.shape[1]), lambda i, *_: (i, 0)),
        column_block(1),
        whole(tables[0].shape),
        whole(tables[1].shape),
    ]


def gate_late(queries, keys_in, values_in, short_taps, filters, skip_gain, tables):
    rows, channels = queries.shape
    out_rows = rows - EARLY * BLK
    return pl.pallas_call(
        functools.partial(late_kernel, EARLY),
        grid=(channels // WIDTH,),
        out_shape=jax.ShapeDtypeStruct((out_rows, channels), jnp.bfloat16),
        in_specs=[column_block(rows)] * 3 + parameter_specs(short_taps, filters, tables),
        out_specs=column_block(out_rows),
        scratch_shapes=[pltpu.VMEM((out_rows + BLK, WIDTH), jnp.bfloat16)],
        compiler_params=pltpu.CompilerParams(vmem_limit_bytes=VMEM_LIMIT),
        cost_estimate=pl.CostEstimate(flops=4 * 10**9, bytes_accessed=3 * 10**6, transcendentals=0),
        name="gate_late",
    )(*map(stay, (queries, keys_in, values_in, short_taps, filters, skip_gain, *tables)))


def gate_early(place, queries, keys_in, values_in, halo, late, short_taps, filters, skip_gain, tables):
    rows, channels = queries.shape
    half = jax.ShapeDtypeStruct((rows // 2, channels), jnp.bfloat16)
    return pl.pallas_call(
        early_kernel,
        grid_spec=pltpu.PrefetchScalarGridSpec(
            num_scalar_prefetch=2,
            grid=(channels // WIDTH,),
            in_specs=[column_block(EARLY * BLK)] * 3
            + [column_block(halo.shape[0]), column_block(late.shape[0])]
            + parameter_specs(short_taps, filters, tables),
            out_specs=[column_block(rows // 2)] * 2,
            scratch_shapes=[
                pltpu.VMEM(((EARLY + 1) * BLK, WIDTH), jnp.bfloat16),
                pltpu.VMEM((rows, WIDTH), jnp.bfloat16),
            ],
        ),
        out_shape=[half, half],
        compiler_params=pltpu.CompilerParams(vmem_limit_bytes=VMEM_LIMIT),
        cost_estimate=pl.CostEstimate(flops=2 * 10**9, bytes_accessed=3 * 10**6, transcendentals=0),
        name="gate_early",
    )(
        place,
        jnp.asarray(row_order()),
        *map(stay, (queries, keys_in, values_in)),
        halo,
        late,
        *map(stay, (short_taps, filters, skip_gain, *tables)),
    )


def scatter_rows(acc, refs, pieces):
    acc = acc.astype(jnp.bfloat16)
    for ref, spans in zip(refs, pieces):
        at = 0
        for start, stop in spans:
            ref[at : at + stop - start] = acc[start:stop]
            at += stop - start


def both_products(a_ref, b_ref, wa_ref, wb_ref):
    acc = jnp.dot(a_ref[...], wa_ref[...], preferred_element_type=jnp.float32)
    return acc + jnp.dot(b_ref[...], wb_ref[...], preferred_element_type=jnp.float32)


def own_kernel(a_ref, wa_ref, part_ref):
    part_ref[...] = jnp.dot(a_ref[...], wa_ref[...], preferred_element_type=jnp.float32)


def rest_kernel(pieces, b_ref, wb_ref, part_ref, *out_refs):
    acc = part_ref[...] + jnp.dot(b_ref[...], wb_ref[...], preferred_element_type=jnp.float32)
    scatter_rows(acc, out_refs, pieces)


def project_kernel(pieces, half, a_ref, b_ref, wa_ref, wb_ref, *out_refs):
    acc = both_products(a_ref, b_ref, wa_ref, wb_ref)
    if half is None:
        scatter_rows(acc, out_refs, pieces)
        return
    j = pl.program_id(0)

    @pl.when(j < half)
    def _():
        scatter_rows(acc, out_refs[: len(pieces)], pieces)

    @pl.when(j >= half)
    def _():
        scatter_rows(acc, out_refs[len(pieces) :], pieces)


def project_call(kernel, operands, specs, out_shape, out_specs, count, tile, depth, name):
    rows = operands[0].shape[0]
    return pl.pallas_call(
        kernel,
        grid=(count // tile,),
        out_shape=out_shape,
        in_specs=specs,
        out_specs=out_specs,
        compiler_params=pltpu.CompilerParams(vmem_limit_bytes=VMEM_LIMIT),
        cost_estimate=pl.CostEstimate(
            flops=2 * rows * depth * count, bytes_accessed=2 * (depth + rows) * count, transcendentals=0
        ),
        name=name,
    )(*operands)


def weight_block(depth, first, tile):
    return pl.BlockSpec((depth, tile), lambda j: (0, j + first // tile))


def row_sizes(pieces):
    return [sum(stop - start for start, stop in spans) for spans in pieces]


def project_own(mine, weight, first, count, tile):
    rows, depth = mine.shape
    return project_call(
        own_kernel,
        (mine, stay(weight)),
        [pl.BlockSpec((rows, depth), lambda j: (0, 0)), weight_block(depth, first, tile)],
        jax.ShapeDtypeStruct((rows, count), jnp.float32),
        pl.BlockSpec((rows, tile), lambda j: (0, j)),
        count,
        tile,
        depth,
        "project_own",
    )


def project_rest(theirs, weight_pair, part, first, tile, pieces):
    rows, depth = theirs.shape
    count = part.shape[1]
    return project_call(
        functools.partial(rest_kernel, pieces),
        (theirs, stay(weight_pair), part),
        [
            pl.BlockSpec((rows, depth), lambda j: (0, 0)),
            weight_block(depth, first, tile),
            pl.BlockSpec((rows, tile), lambda j: (0, j)),
        ],
        [jax.ShapeDtypeStruct((n, count), jnp.bfloat16) for n in row_sizes(pieces)],
        [pl.BlockSpec((n, tile), lambda j: (0, j)) for n in row_sizes(pieces)],
        count,
        tile,
        depth,
        "project_rest",
    )


def project(mine, theirs, weight, weight_pair, first, count, tile, pieces, halves=False):
    rows, depth = mine.shape
    lhs = pl.BlockSpec((rows, depth), lambda j: (0, 0))
    rhs = weight_block(depth, first, tile)
    sizes = row_sizes(pieces)
    if halves:
        half = count // tile // 2
        shapes = [jax.ShapeDtypeStruct((n, count // 2), jnp.bfloat16) for n in sizes] * 2
        out_specs = [pl.BlockSpec((n, tile), lambda j: (0, jnp.minimum(j, half - 1))) for n in sizes]
        out_specs += [pl.BlockSpec((n, tile), lambda j: (0, jnp.maximum(j - half, 0))) for n in sizes]
    else:
        half = None
        shapes = [jax.ShapeDtypeStruct((n, count), jnp.bfloat16) for n in sizes]
        out_specs = [pl.BlockSpec((n, tile), lambda j: (0, j)) for n in sizes]
    return project_call(
        functools.partial(project_kernel, pieces, half),
        (mine, theirs, stay(weight), stay(weight_pair)),
        [lhs, lhs, rhs, rhs],
        shapes,
        out_specs,
        count,
        tile,
        2 * depth,
        "project",
    )


def moved(dy=0, dx=0, dc=0):
    pairs = []
    for y in range(N_Y):
        for x in range(N_X):
            for c in range(N_C):
                source = (y * N_X + x) * N_C + c
                target = (((y + dy) % N_Y) * N_X + (x + dx) % N_X) * N_C + (c + dc) % N_C
                pairs.append((source, target))
    return pairs


def send(array, **step):
    return lax.ppermute(array, "tp", moved(**step))


def add(*arrays):
    total = arrays[0].astype(jnp.float32)
    for array in arrays[1:]:
        total = total + array.astype(jnp.float32)
    return total


X_FIRST = (2304, 1280)


def body(queries, keys_in, values_in, short_taps, filters, skip_gain, out_weight, residual):
    rows = queries.shape[0]
    width = out_weight.shape[1]
    peers = lax.axis_size("ctx")
    piece = rows // (N_Y * N_X * N_C)
    weight_pair = send(out_weight, dc=1)
    rim = make_rim(queries, keys_in, values_in, short_taps)
    halo = lax.ppermute(rim, "ctx", [(i, i + 1) for i in range(peers - 1)])
    parameters = (short_taps, filters, skip_gain[None, :], transform_tables(filters.shape[1]))
    late = gate_late(queries, keys_in, values_in, *parameters)
    place = lax.axis_index("tp").astype(jnp.int32)[None]
    keep, give = gate_early(place, queries, keys_in, values_in, halo, late, *parameters)
    theirs = send(give, dc=1)

    half = rows // (2 * N_C)
    by_x = (((0, half),), ((half, 2 * half),))
    by_y = tuple(((s * piece, (s + 1) * piece), (half + s * piece, half + (s + 1) * piece)) for s in range(N_Y))

    def narrow(array):
        return array.astype(jnp.bfloat16)

    y_first = width - sum(X_FIRST)
    tile = y_first // 4
    a0_part = project_own(keep, out_weight, y_first, X_FIRST[0], tile)
    a0_keep, a0_give = project_rest(theirs, weight_pair, a0_part, y_first, tile, by_x)
    a0_got = send(a0_give, dx=1)
    left = lax.optimization_barrier((keep, a0_keep))[0]
    b_all = project(left, theirs, out_weight, weight_pair, 0, y_first, tile, by_y, halves=True)
    b0, b1 = b_all[:N_Y], b_all[N_Y:]
    left = lax.optimization_barrier((keep, b0[0]))[0]
    last = width - X_FIRST[1]
    a1_keep, a1_give = project(
        left, theirs, out_weight, weight_pair, last, X_FIRST[1], math.gcd(last, X_FIRST[1]), by_x
    )

    b1_far = send(b1[2], dy=1)
    b0_far = send(b0[2], dy=-1)
    b0_up = send(b0[1], dy=1)
    b1_down = send(b1[3], dy=-1)
    a1_got = send(lax.optimization_barrier((a1_give, a0_got))[0], dx=1)

    b0_far, b1_far, a0_got = lax.optimization_barrier((b0_far, b1_far, a0_got))
    b1_up = send(narrow(add(b1[1], b1_far)), dy=1)
    b0_down = send(narrow(add(b0[3], b0_far)), dy=-1)

    a0, a1 = add(a0_keep, a0_got), add(a1_keep, a1_got)
    edge = sum(X_FIRST) // 2
    low = [a0[s * piece : (s + 1) * piece, :edge] for s in range(N_Y)]
    high = [
        jnp.concatenate([a0[s * piece : (s + 1) * piece, edge:], a1[s * piece : (s + 1) * piece]], axis=1)
        for s in range(N_Y)
    ]
    low_send, high_send = [narrow(part) for part in low], [narrow(part) for part in high]
    low_send, high_send, b0_up, b1_down = lax.optimization_barrier((low_send, high_send, b0_up, b1_down))
    low_far = send(low_send[2], dy=-1)
    high_far = send(high_send[2], dy=1)

    b0_sum, b1_sum = add(b0[0], b0_up, b0_down), add(b1[0], b1_up, b1_down)
    b0_give, b1_give = narrow(b0_sum[piece:]), narrow(b1_sum[piece:])
    b0_got = send(b0_give, dx=1)
    low_up = send(low_send[1], dy=1)
    high_down = send(high_send[3], dy=-1)

    low_far, high_far, b1_give = lax.optimization_barrier((low_far, high_far, b1_give))
    low_down = send(narrow(add(low[3], low_far)), dy=-1)
    high_up = send(narrow(add(high[1], high_far)), dy=1)
    b1_got = send(b1_give, dx=1)

    summed = jnp.concatenate(
        [
            add(b0_sum[:piece], b0_got),
            add(b1_sum[:piece], b1_got),
            add(low[0], low_up, low_down),
            add(high[0], high_down, high_up),
        ],
        axis=1,
    )
    return narrow(residual.astype(jnp.float32) + summed)


def solution(mesh):
    in_specs = (
        P("ctx", "tp"),
        P("ctx", "tp"),
        P("ctx", "tp"),
        P(None, "tp"),
        P("tp", None),
        P("tp"),
        P("tp", None),
        P(("ctx", "tp"), None),
    )
    out_specs = P(("ctx", "tp"), None)
    return jax.shard_map(body, mesh=mesh, in_specs=in_specs, out_specs=out_specs, check_vma=False)
```

```python
import math
import functools
import numpy as np
import jax
import jax.numpy as jnp
from jax import lax
from jax.experimental import pallas as pl
from jax.experimental.pallas import tpu as pltpu
from jax.sharding import PartitionSpec as P

BLK = 128
N_Y, N_X, N_C = 4, 2, 2


def split_bf16(matrix):
    high = matrix.astype(jnp.bfloat16)
    low = (matrix - high.astype(np.float64)).astype(jnp.bfloat16)
    return high, low


def transform_tables(taps):
    span = 2 * taps
    freq = np.arange(taps)[:, None] + 0.5
    time = np.arange(span)[None, :]
    angle = 2.0 * np.pi * freq * time / span
    forward = np.concatenate([np.cos(angle), -np.sin(angle)], axis=0)
    inverse = (2.0 / span) * forward.T[taps:]
    f_high, f_low = split_bf16(forward)
    g_high, g_low = split_bf16(inverse)
    return np.concatenate([f_high, f_low], axis=0), np.concatenate([g_high, g_low], axis=0)


def short_filter(wide, taps):
    rows = wide.shape[0] - 16
    total = taps[0:1] * wide[16 : 16 + rows]
    for j in range(1, taps.shape[0]):
        total = total + taps[j : j + 1] * wide[16 - j : 16 - j + rows]
    return total


def spectrum(f_ref, filt_ref):
    spec = lax.dot_general(
        f_ref[:, :BLK], filt_ref[...], (((1,), (1,)), ((), ())), preferred_element_type=jnp.float32
    )
    spec = spec[: 2 * BLK] + spec[2 * BLK :]
    return spec[:BLK], spec[BLK:]


def long_filter(span, h_re, h_im, f_ref, g_ref):
    x = jnp.dot(f_ref[...], span, preferred_element_type=jnp.float32)
    x = x[: 2 * BLK] + x[2 * BLK :]
    x_re, x_im = x[:BLK], x[BLK:]
    y = jnp.concatenate([x_re * h_re - x_im * h_im, x_re * h_im + x_im * h_re], axis=0)
    y_high = y.astype(jnp.bfloat16)
    y_low = (y - y_high.astype(jnp.float32)).astype(jnp.bfloat16)
    z = jnp.dot(g_ref[...], y_high, preferred_element_type=jnp.float32)
    return z[:BLK] + z[BLK:] + jnp.dot(g_ref[:BLK], y_low, preferred_element_type=jnp.float32)


def window(ref, b):
    return ref[b * BLK - 16 : (b + 1) * BLK].astype(jnp.float32)


def rim_kernel(q_ref, k_ref, v_ref, taps_ref, out_ref):
    taps = taps_ref[...].astype(jnp.float32)
    tail = BLK + 16
    at = k_ref.shape[0] - tail
    k_win, v_win = k_ref[at:].astype(jnp.float32), v_ref[at:].astype(jnp.float32)
    out_ref[:BLK] = (short_filter(k_win, taps) * short_filter(v_win, taps)).astype(jnp.bfloat16)
    q_end = pltpu.roll(q_ref[...].astype(jnp.float32), 2, 0)
    k_end = pltpu.roll(k_win[BLK:], 4, 0)
    v_end = pltpu.roll(v_win[BLK:], 6, 0)
    row = lax.broadcasted_iota(jnp.int32, q_end.shape, 0)
    packed = jnp.where(row < 2, q_end, jnp.where(row < 4, k_end, v_end))
    out_ref[BLK:] = packed.astype(jnp.bfloat16)


def late_kernel(first, q_ref, k_ref, v_ref, taps_ref, filt_ref, skip_ref, f_ref, g_ref, out_ref, prod_ref):
    blocks = q_ref.shape[0] // BLK
    taps = taps_ref[...].astype(jnp.float32)
    skip = skip_ref[...]
    h_re, h_im = spectrum(f_ref, filt_ref)
    for b in range(first - 1, blocks):
        at = (b - first + 1) * BLK
        prod = short_filter(window(k_ref, b), taps) * short_filter(window(v_ref, b), taps)
        prod = prod.astype(jnp.bfloat16)
        prod_ref[at : at + BLK] = prod
        if b >= first:
            filtered = long_filter(prod_ref[at - BLK : at + BLK], h_re, h_im, f_ref, g_ref)
            gated = short_filter(window(q_ref, b), taps) * (filtered + skip * prod.astype(jnp.float32))
            out_ref[at - BLK : at] = gated.astype(jnp.bfloat16)


def early_kernel(
    place_ref, order_ref, q_ref, k_ref, v_ref, halo_ref, late_ref, taps_ref, filt_ref, skip_ref, f_ref, g_ref,
    keep_ref, give_ref, prod_ref, gated_ref,
):
    blocks = q_ref.shape[0] // BLK
    taps = taps_ref[...].astype(jnp.float32)
    skip = skip_ref[...]
    rim = halo_ref[BLK:].astype(jnp.float32)

    def rows_of(ref, b, turn):
        if b == 0:
            return jnp.concatenate([pltpu.roll(rim, turn, 0), ref[:BLK].astype(jnp.float32)], axis=0)
        return window(ref, b)

    h_re, h_im = spectrum(f_ref, filt_ref)
    prod_ref[:BLK] = halo_ref[:BLK]
    for b in range(blocks):
        prod = short_filter(rows_of(k_ref, b, 12), taps) * short_filter(rows_of(v_ref, b, 10), taps)
        prod = prod.astype(jnp.bfloat16)
        prod_ref[(b + 1) * BLK : (b + 2) * BLK] = prod
        filtered = long_filter(prod_ref[b * BLK : (b + 2) * BLK], h_re, h_im, f_ref, g_ref)
        gated = short_filter(rows_of(q_ref, b, 14), taps) * (filtered + skip * prod.astype(jnp.float32))
        gated_ref[b * BLK : (b + 1) * BLK] = gated.astype(jnp.bfloat16)
    gated_ref[blocks * BLK :] = late_ref[...]

    slots = N_Y * N_X
    piece = keep_ref.shape[0] // slots
    for slot in range(slots):
        for which, ref in ((0, keep_ref), (1, give_ref)):
            group = order_ref[(place_ref[0] * 2 + which) * slots + slot]
            start = pl.multiple_of(group * piece, 16)
            ref[slot * piece : (slot + 1) * piece] = gated_ref[pl.ds(start, piece)]


def row_order():
    table = []
    for y in range(N_Y):
        for x in range(N_X):
            for c in range(N_C):
                for dc in range(N_C):
                    for dx in range(N_X):
                        for dy in range(N_Y):
                            table.append((((y + dy) % N_Y) * N_X + (x + dx) % N_X) * N_C + (c + dc) % N_C)
    return np.array(table, np.int32)


VMEM_LIMIT = 24 * 1024 * 1024
EARLY = 2
WIDTH = 256


def stay(array):
    return pltpu.with_memory_space_constraint(array, pltpu.HBM)


def column_block(rows, index=0):
    return pl.BlockSpec((rows, WIDTH), lambda i, *_: (index, i))


def whole(shape):
    return pl.BlockSpec(shape, lambda i, *_: (0, 0))


def make_rim(queries, keys_in, values_in, short_taps):
    rows, channels = queries.shape
    part = rows // 4
    return pl.pallas_call(
        rim_kernel,
        grid=(channels // WIDTH,),
        out_shape=jax.ShapeDtypeStruct((BLK + 16, channels), jnp.bfloat16),
        in_specs=[
            column_block(16, rows // 16 - 1),
            column_block(part, rows // part - 1),
            column_block(part, rows // part - 1),
            column_block(short_taps.shape[0]),
        ],
        out_specs=column_block(BLK + 16),
        compiler_params=pltpu.CompilerParams(vmem_limit_bytes=VMEM_LIMIT),
        cost_estimate=pl.CostEstimate(flops=10**9, bytes_accessed=10**6, transcendentals=0),
        name="rim",
    )(stay(queries), stay(keys_in), stay(values_in), stay(short_taps))


def parameter_specs(short_taps, filters, tables):
    return [
        column_block(short_taps.shape[0]),
        pl.BlockSpec((WIDTH, filters.shape[1]), lambda i, *_: (i, 0)),
        column_block(1),
        whole(tables[0].shape),
        whole(tables[1].shape),
    ]


def gate_late(queries, keys_in, values_in, short_taps, filters, skip_gain, tables):
    rows, channels = queries.shape
    out_rows = rows - EARLY * BLK
    return pl.pallas_call(
        functools.partial(late_kernel, EARLY),
        grid=(channels // WIDTH,),
        out_shape=jax.ShapeDtypeStruct((out_rows, channels), jnp.bfloat16),
        in_specs=[column_block(rows)] * 3 + parameter_specs(short_taps, filters, tables),
        out_specs=column_block(out_rows),
        scratch_shapes=[pltpu.VMEM((out_rows + BLK, WIDTH), jnp.bfloat16)],
        compiler_params=pltpu.CompilerParams(vmem_limit_bytes=VMEM_LIMIT),
        cost_estimate=pl.CostEstimate(flops=4 * 10**9, bytes_accessed=3 * 10**6, transcendentals=0),
        name="gate_late",
    )(*map(stay, (queries, keys_in, values_in, short_taps, filters, skip_gain, *tables)))


def gate_early(place, queries, keys_in, values_in, halo, late, short_taps, filters, skip_gain, tables):
    rows, channels = queries.shape
    half = jax.ShapeDtypeStruct((rows // 2, channels), jnp.bfloat16)
    return pl.pallas_call(
        early_kernel,
        grid_spec=pltpu.PrefetchScalarGridSpec(
            num_scalar_prefetch=2,
            grid=(channels // WIDTH,),
            in_specs=[column_block(EARLY * BLK)] * 3
            + [column_block(halo.shape[0]), column_block(late.shape[0])]
            + parameter_specs(short_taps, filters, tables),
            out_specs=[column_block(rows // 2)] * 2,
            scratch_shapes=[
                pltpu.VMEM(((EARLY + 1) * BLK, WIDTH), jnp.bfloat16),
                pltpu.VMEM((rows, WIDTH), jnp.bfloat16),
            ],
        ),
        out_shape=[half, half],
        compiler_params=pltpu.CompilerParams(vmem_limit_bytes=VMEM_LIMIT),
        cost_estimate=pl.CostEstimate(flops=2 * 10**9, bytes_accessed=3 * 10**6, transcendentals=0),
        name="gate_early",
    )(
        place,
        jnp.asarray(row_order()),
        *map(stay, (queries, keys_in, values_in)),
        halo,
        late,
        *map(stay, (short_taps, filters, skip_gain, *tables)),
    )


def scatter_rows(acc, refs, pieces):
    acc = acc.astype(jnp.bfloat16)
    for ref, spans in zip(refs, pieces):
        at = 0
        for start, stop in spans:
            ref[at : at + stop - start] = acc[start:stop]
            at += stop - start


def both_products(a_ref, b_ref, wa_ref, wb_ref):
    acc = jnp.dot(a_ref[...], wa_ref[...], preferred_element_type=jnp.float32)
    return acc + jnp.dot(b_ref[...], wb_ref[...], preferred_element_type=jnp.float32)


def own_kernel(a_ref, wa_ref, part_ref):
    part_ref[...] = jnp.dot(a_ref[...], wa_ref[...], preferred_element_type=jnp.float32)


def rest_kernel(pieces, b_ref, wb_ref, part_ref, *out_refs):
    acc = part_ref[...] + jnp.dot(b_ref[...], wb_ref[...], preferred_element_type=jnp.float32)
    scatter_rows(acc, out_refs, pieces)


def project_kernel(pieces, half, a_ref, b_ref, wa_ref, wb_ref, *out_refs):
    acc = both_products(a_ref, b_ref, wa_ref, wb_ref)
    if half is None:
        scatter_rows(acc, out_refs, pieces)
        return
    j = pl.program_id(0)

    @pl.when(j < half)
    def _():
        scatter_rows(acc, out_refs[: len(pieces)], pieces)

    @pl.when(j >= half)
    def _():
        scatter_rows(acc, out_refs[len(pieces) :], pieces)


def project_call(kernel, operands, specs, out_shape, out_specs, count, tile, depth, name):
    rows = operands[0].shape[0]
    return pl.pallas_call(
        kernel,
        grid=(count // tile,),
        out_shape=out_shape,
        in_specs=specs,
        out_specs=out_specs,
        compiler_params=pltpu.CompilerParams(vmem_limit_bytes=VMEM_LIMIT),
        cost_estimate=pl.CostEstimate(
            flops=2 * rows * depth * count, bytes_accessed=2 * (depth + rows) * count, transcendentals=0
        ),
        name=name,
    )(*operands)


def weight_block(depth, first, tile):
    return pl.BlockSpec((depth, tile), lambda j: (0, j + first // tile))


def row_sizes(pieces):
    return [sum(stop - start for start, stop in spans) for spans in pieces]


def project_own(mine, weight, first, count, tile):
    rows, depth = mine.shape
    return project_call(
        own_kernel,
        (mine, stay(weight)),
        [pl.BlockSpec((rows, depth), lambda j: (0, 0)), weight_block(depth, first, tile)],
        jax.ShapeDtypeStruct((rows, count), jnp.float32),
        pl.BlockSpec((rows, tile), lambda j: (0, j)),
        count,
        tile,
        depth,
        "project_own",
    )


def project_rest(theirs, weight_pair, part, first, tile, pieces):
    rows, depth = theirs.shape
    count = part.shape[1]
    return project_call(
        functools.partial(rest_kernel, pieces),
        (theirs, stay(weight_pair), part),
        [
            pl.BlockSpec((rows, depth), lambda j: (0, 0)),
            weight_block(depth, first, tile),
            pl.BlockSpec((rows, tile), lambda j: (0, j)),
        ],
        [jax.ShapeDtypeStruct((n, count), jnp.bfloat16) for n in row_sizes(pieces)],
        [pl.BlockSpec((n, tile), lambda j: (0, j)) for n in row_sizes(pieces)],
        count,
        tile,
        depth,
        "project_rest",
    )


def project(mine, theirs, weight, weight_pair, first, count, tile, pieces, halves=False):
    rows, depth = mine.shape
    lhs = pl.BlockSpec((rows, depth), lambda j: (0, 0))
    rhs = weight_block(depth, first, tile)
    sizes = row_sizes(pieces)
    if halves:
        half = count // tile // 2
        shapes = [jax.ShapeDtypeStruct((n, count // 2), jnp.bfloat16) for n in sizes] * 2
        out_specs = [pl.BlockSpec((n, tile), lambda j: (0, jnp.minimum(j, half - 1))) for n in sizes]
        out_specs += [pl.BlockSpec((n, tile), lambda j: (0, jnp.maximum(j - half, 0))) for n in sizes]
    else:
        half = None
        shapes = [jax.ShapeDtypeStruct((n, count), jnp.bfloat16) for n in sizes]
        out_specs = [pl.BlockSpec((n, tile), lambda j: (0, j)) for n in sizes]
    return project_call(
        functools.partial(project_kernel, pieces, half),
        (mine, theirs, stay(weight), stay(weight_pair)),
        [lhs, lhs, rhs, rhs],
        shapes,
        out_specs,
        count,
        tile,
        2 * depth,
        "project",
    )


def moved(dy=0, dx=0, dc=0):
    pairs = []
    for y in range(N_Y):
        for x in range(N_X):
            for c in range(N_C):
                source = (y * N_X + x) * N_C + c
                target = (((y + dy) % N_Y) * N_X + (x + dx) % N_X) * N_C + (c + dc) % N_C
                pairs.append((source, target))
    return pairs


def send(array, **step):
    return lax.ppermute(array, "tp", moved(**step))


def add(*arrays):
    total = arrays[0].astype(jnp.float32)
    for array in arrays[1:]:
        total = total + array.astype(jnp.float32)
    return total


X_FIRST = (2304, 1280)


def body(queries, keys_in, values_in, short_taps, filters, skip_gain, out_weight, residual):
    rows = queries.shape[0]
    width = out_weight.shape[1]
    peers = lax.axis_size("ctx")
    piece = rows // (N_Y * N_X * N_C)
    weight_pair = send(out_weight, dc=1)
    rim = make_rim(queries, keys_in, values_in, short_taps)
    halo = lax.ppermute(rim, "ctx", [(i, i + 1) for i in range(peers - 1)])
    parameters = (short_taps, filters, skip_gain[None, :], transform_tables(filters.shape[1]))
    late = gate_late(queries, keys_in, values_in, *parameters)
    place = lax.axis_index("tp").astype(jnp.int32)[None]
    keep, give = gate_early(place, queries, keys_in, values_in, halo, late, *parameters)
    theirs = send(give, dc=1)

    half = rows // (2 * N_C)
    by_x = (((0, half),), ((half, 2 * half),))
    by_y = tuple(((s * piece, (s + 1) * piece), (half + s * piece, half + (s + 1) * piece)) for s in range(N_Y))

    def narrow(array):
        return array.astype(jnp.bfloat16)

    y_first = width - sum(X_FIRST)
    tile = y_first // 4
    a0_part = project_own(keep, out_weight, y_first, X_FIRST[0], tile)
    a0_keep, a0_give = project_rest(theirs, weight_pair, a0_part, y_first, tile, by_x)
    a0_got = send(a0_give, dx=1)
    left = lax.optimization_barrier((keep, a0_keep))[0]
    b_all = project(left, theirs, out_weight, weight_pair, 0, y_first, y_first // 2, by_y, halves=True)
    b0, b1 = b_all[:N_Y], b_all[N_Y:]
    left = lax.optimization_barrier((keep, b0[0]))[0]
    last = width - X_FIRST[1]
    a1_keep, a1_give = project(
        left, theirs, out_weight, weight_pair, last, X_FIRST[1], math.gcd(last, X_FIRST[1]), by_x
    )

    b1_far = send(b1[2], dy=1)
    b0_far = send(b0[2], dy=-1)
    b0_up = send(b0[1], dy=1)
    b1_down = send(b1[3], dy=-1)
    a1_got = send(lax.optimization_barrier((a1_give, a0_got))[0], dx=1)

    b0_far, b1_far, a0_got = lax.optimization_barrier((b0_far, b1_far, a0_got))
    b1_up = send(narrow(add(b1[1], b1_far)), dy=1)
    b0_down = send(narrow(add(b0[3], b0_far)), dy=-1)

    a0, a1 = add(a0_keep, a0_got), add(a1_keep, a1_got)
    edge = sum(X_FIRST) // 2
    low = [a0[s * piece : (s + 1) * piece, :edge] for s in range(N_Y)]
    high = [
        jnp.concatenate([a0[s * piece : (s + 1) * piece, edge:], a1[s * piece : (s + 1) * piece]], axis=1)
        for s in range(N_Y)
    ]
    low_send, high_send = [narrow(part) for part in low], [narrow(part) for part in high]
    low_send, high_send, b0_up, b1_down = lax.optimization_barrier((low_send, high_send, b0_up, b1_down))
    low_far = send(low_send[2], dy=-1)
    high_far = send(high_send[2], dy=1)

    b0_sum, b1_sum = add(b0[0], b0_up, b0_down), add(b1[0], b1_up, b1_down)
    b0_give, b1_give = narrow(b0_sum[piece:]), narrow(b1_sum[piece:])
    b0_got = send(b0_give, dx=1)

    low_far, high_far = lax.optimization_barrier((low_far, high_far))
    down = send(jnp.concatenate([narrow(add(low[3], low_far)), high_send[3]], axis=1), dy=-1)
    up = send(jnp.concatenate([low_send[1], narrow(add(high[1], high_far))], axis=1), dy=1)
    b1_got = send(lax.optimization_barrier((b1_give, low_far, high_far, b0_got))[0], dx=1)

    summed = jnp.concatenate(
        [
            add(b0_sum[:piece], b0_got),
            add(b1_sum[:piece], b1_got),
            add(jnp.concatenate([low[0], high[0]], axis=1), up, down),
        ],
        axis=1,
    )
    return narrow(residual.astype(jnp.float32) + summed)


def solution(mesh):
    in_specs = (
        P("ctx", "tp"),
        P("ctx", "tp"),
        P("ctx", "tp"),
        P(None, "tp"),
        P("tp", None),
        P("tp"),
        P("tp", None),
        P(("ctx", "tp"), None),
    )
    out_specs = P(("ctx", "tp"), None)
    return jax.shard_map(body, mesh=mesh, in_specs=in_specs, out_specs=out_specs, check_vma=False)
```

```python
import math
import functools
import numpy as np
import jax
import jax.numpy as jnp
from jax import lax
from jax.experimental import pallas as pl
from jax.experimental.pallas import tpu as pltpu
from jax.sharding import PartitionSpec as P

BLK = 128
N_Y, N_X, N_C = 4, 2, 2


def split_bf16(matrix):
    high = matrix.astype(jnp.bfloat16)
    low = (matrix - high.astype(np.float64)).astype(jnp.bfloat16)
    return high, low


def transform_tables(taps):
    span = 2 * taps
    freq = np.arange(taps)[:, None] + 0.5
    time = np.arange(span)[None, :]
    angle = 2.0 * np.pi * freq * time / span
    forward = np.concatenate([np.cos(angle), -np.sin(angle)], axis=0)
    inverse = (2.0 / span) * forward.T[taps:]
    f_high, f_low = split_bf16(forward)
    g_high, g_low = split_bf16(inverse)
    return np.concatenate([f_high, f_low], axis=0), np.concatenate([g_high, g_low], axis=0)


def short_filter(wide, taps):
    rows = wide.shape[0] - 16
    total = taps[0:1] * wide[16 : 16 + rows]
    for j in range(1, taps.shape[0]):
        total = total + taps[j : j + 1] * wide[16 - j : 16 - j + rows]
    return total


def spectrum(f_ref, filt_ref):
    spec = lax.dot_general(
        f_ref[:, :BLK], filt_ref[...], (((1,), (1,)), ((), ())), preferred_element_type=jnp.float32
    )
    spec = spec[: 2 * BLK] + spec[2 * BLK :]
    return spec[:BLK], spec[BLK:]


def long_filter(span, h_re, h_im, f_ref, g_ref):
    x = jnp.dot(f_ref[...], span, preferred_element_type=jnp.float32)
    x = x[: 2 * BLK] + x[2 * BLK :]
    x_re, x_im = x[:BLK], x[BLK:]
    y = jnp.concatenate([x_re * h_re - x_im * h_im, x_re * h_im + x_im * h_re], axis=0)
    y_high = y.astype(jnp.bfloat16)
    y_low = (y - y_high.astype(jnp.float32)).astype(jnp.bfloat16)
    z = jnp.dot(g_ref[...], y_high, preferred_element_type=jnp.float32)
    return z[:BLK] + z[BLK:] + jnp.dot(g_ref[:BLK], y_low, preferred_element_type=jnp.float32)


def window(ref, b):
    return ref[b * BLK - 16 : (b + 1) * BLK].astype(jnp.float32)


def rim_kernel(q_ref, k_ref, v_ref, taps_ref, out_ref):
    taps = taps_ref[...].astype(jnp.float32)
    tail = BLK + 16
    at = k_ref.shape[0] - tail
    k_win, v_win = k_ref[at:].astype(jnp.float32), v_ref[at:].astype(jnp.float32)
    out_ref[:BLK] = (short_filter(k_win, taps) * short_filter(v_win, taps)).astype(jnp.bfloat16)
    q_end = pltpu.roll(q_ref[...].astype(jnp.float32), 2, 0)
    k_end = pltpu.roll(k_win[BLK:], 4, 0)
    v_end = pltpu.roll(v_win[BLK:], 6, 0)
    row = lax.broadcasted_iota(jnp.int32, q_end.shape, 0)
    packed = jnp.where(row < 2, q_end, jnp.where(row < 4, k_end, v_end))
    out_ref[BLK:] = packed.astype(jnp.bfloat16)


def late_kernel(first, q_ref, k_ref, v_ref, taps_ref, filt_ref, skip_ref, f_ref, g_ref, out_ref, spec_ref, prod_ref):
    blocks = q_ref.shape[0] // BLK
    taps = taps_ref[...].astype(jnp.float32)
    skip = skip_ref[...]
    h_re, h_im = spectrum(f_ref, filt_ref)
    spec_ref[:BLK] = h_re
    spec_ref[BLK:] = h_im
    for b in range(first - 1, blocks):
        at = (b - first + 1) * BLK
        prod = short_filter(window(k_ref, b), taps) * short_filter(window(v_ref, b), taps)
        prod = prod.astype(jnp.bfloat16)
        prod_ref[at : at + BLK] = prod
        if b >= first:
            filtered = long_filter(prod_ref[at - BLK : at + BLK], h_re, h_im, f_ref, g_ref)
            gated = short_filter(window(q_ref, b), taps) * (filtered + skip * prod.astype(jnp.float32))
            out_ref[at - BLK : at] = gated.astype(jnp.bfloat16)


def early_kernel(
    place_ref, order_ref, q_ref, k_ref, v_ref, halo_ref, late_ref, spec_ref, taps_ref, skip_ref, f_ref, g_ref,
    keep_ref, give_ref, prod_ref, gated_ref,
):
    blocks = q_ref.shape[0] // BLK
    taps = taps_ref[...].astype(jnp.float32)
    skip = skip_ref[...]
    rim = halo_ref[BLK:].astype(jnp.float32)

    def rows_of(ref, b, turn):
        if b == 0:
            return jnp.concatenate([pltpu.roll(rim, turn, 0), ref[:BLK].astype(jnp.float32)], axis=0)
        return window(ref, b)

    h_re, h_im = spec_ref[:BLK], spec_ref[BLK:]
    prod_ref[:BLK] = halo_ref[:BLK]
    for b in range(blocks):
        prod = short_filter(rows_of(k_ref, b, 12), taps) * short_filter(rows_of(v_ref, b, 10), taps)
        prod = prod.astype(jnp.bfloat16)
        prod_ref[(b + 1) * BLK : (b + 2) * BLK] = prod
        filtered = long_filter(prod_ref[b * BLK : (b + 2) * BLK], h_re, h_im, f_ref, g_ref)
        gated = short_filter(rows_of(q_ref, b, 14), taps) * (filtered + skip * prod.astype(jnp.float32))
        gated_ref[b * BLK : (b + 1) * BLK] = gated.astype(jnp.bfloat16)
    gated_ref[blocks * BLK :] = late_ref[...]

    slots = N_Y * N_X
    piece = keep_ref.shape[0] // slots
    for slot in range(slots):
        for which, ref in ((0, keep_ref), (1, give_ref)):
            group = order_ref[(place_ref[0] * 2 + which) * slots + slot]
            start = pl.multiple_of(group * piece, 16)
            ref[slot * piece : (slot + 1) * piece] = gated_ref[pl.ds(start, piece)]


def row_order():
    table = []
    for y in range(N_Y):
        for x in range(N_X):
            for c in range(N_C):
                for dc in range(N_C):
                    for dx in range(N_X):
                        for dy in range(N_Y):
                            table.append((((y + dy) % N_Y) * N_X + (x + dx) % N_X) * N_C + (c + dc) % N_C)
    return np.array(table, np.int32)


VMEM_LIMIT = 24 * 1024 * 1024
EARLY = 2
WIDTH = 256


def stay(array):
    return pltpu.with_memory_space_constraint(array, pltpu.HBM)


def column_block(rows, index=0, width=WIDTH):
    return pl.BlockSpec((rows, width), lambda i, *_: (index, i))


def whole(shape):
    return pl.BlockSpec(shape, lambda i, *_: (0, 0))


def make_rim(queries, keys_in, values_in, short_taps):
    rows, channels = queries.shape
    part = rows // 4
    return pl.pallas_call(
        rim_kernel,
        grid=(channels // WIDTH,),
        out_shape=jax.ShapeDtypeStruct((BLK + 16, channels), jnp.bfloat16),
        in_specs=[
            column_block(16, rows // 16 - 1),
            column_block(part, rows // part - 1),
            column_block(part, rows // part - 1),
            column_block(short_taps.shape[0]),
        ],
        out_specs=column_block(BLK + 16),
        compiler_params=pltpu.CompilerParams(vmem_limit_bytes=VMEM_LIMIT),
        cost_estimate=pl.CostEstimate(flops=10**9, bytes_accessed=10**6, transcendentals=0),
        name="rim",
    )(stay(queries), stay(keys_in), stay(values_in), stay(short_taps))


def parameter_specs(short_taps, filters, tables):
    return [
        column_block(short_taps.shape[0]),
        pl.BlockSpec((WIDTH, filters.shape[1]), lambda i, *_: (i, 0)),
        column_block(1),
        whole(tables[0].shape),
        whole(tables[1].shape),
    ]


def gate_late(queries, keys_in, values_in, short_taps, filters, skip_gain, tables):
    rows, channels = queries.shape
    out_rows = rows - EARLY * BLK
    return pl.pallas_call(
        functools.partial(late_kernel, EARLY),
        grid=(channels // WIDTH,),
        out_shape=[
            jax.ShapeDtypeStruct((out_rows, channels), jnp.bfloat16),
            jax.ShapeDtypeStruct((2 * BLK, channels), jnp.float32),
        ],
        in_specs=[column_block(rows)] * 3 + parameter_specs(short_taps, filters, tables),
        out_specs=[column_block(out_rows), column_block(2 * BLK)],
        scratch_shapes=[pltpu.VMEM((out_rows + BLK, WIDTH), jnp.bfloat16)],
        compiler_params=pltpu.CompilerParams(vmem_limit_bytes=VMEM_LIMIT),
        cost_estimate=pl.CostEstimate(flops=4 * 10**9, bytes_accessed=3 * 10**6, transcendentals=0),
        name="gate_late",
    )(*map(stay, (queries, keys_in, values_in, short_taps, filters, skip_gain, *tables)))


def gate_early(place, queries, keys_in, values_in, halo, late, spec, short_taps, skip_gain, tables):
    rows, channels = queries.shape
    half = jax.ShapeDtypeStruct((rows // 2, channels), jnp.bfloat16)
    return pl.pallas_call(
        early_kernel,
        grid_spec=pltpu.PrefetchScalarGridSpec(
            num_scalar_prefetch=2,
            grid=(1,),
            in_specs=[
                column_block(n, 0, channels)
                for n in [EARLY * BLK] * 3 + [halo.shape[0], late.shape[0], spec.shape[0], short_taps.shape[0], 1]
            ]
            + [whole(table.shape) for table in tables],
            out_specs=[column_block(rows // 2, 0, channels)] * 2,
            scratch_shapes=[
                pltpu.VMEM(((EARLY + 1) * BLK, channels), jnp.bfloat16),
                pltpu.VMEM((rows, channels), jnp.bfloat16),
            ],
        ),
        out_shape=[half, half],
        compiler_params=pltpu.CompilerParams(vmem_limit_bytes=VMEM_LIMIT),
        cost_estimate=pl.CostEstimate(flops=2 * 10**9, bytes_accessed=3 * 10**6, transcendentals=0),
        name="gate_early",
    )(
        place,
        jnp.asarray(row_order()),
        *map(stay, (queries, keys_in, values_in)),
        halo,
        late,
        spec,
        *map(stay, (short_taps, skip_gain, *tables)),
    )


def scatter_rows(acc, refs, pieces):
    acc = acc.astype(jnp.bfloat16)
    for ref, spans in zip(refs, pieces):
        at = 0
        for start, stop in spans:
            ref[at : at + stop - start] = acc[start:stop]
            at += stop - start


def both_products(a_ref, b_ref, wa_ref, wb_ref):
    acc = jnp.dot(a_ref[...], wa_ref[...], preferred_element_type=jnp.float32)
    return acc + jnp.dot(b_ref[...], wb_ref[...], preferred_element_type=jnp.float32)


def own_kernel(a_ref, wa_ref, part_ref):
    part_ref[...] = jnp.dot(a_ref[...], wa_ref[...], preferred_element_type=jnp.float32)


def rest_kernel(pieces, b_ref, wb_ref, part_ref, *out_refs):
    acc = part_ref[...] + jnp.dot(b_ref[...], wb_ref[...], preferred_element_type=jnp.float32)
    scatter_rows(acc, out_refs, pieces)


def project_kernel(pieces, half, a_ref, b_ref, wa_ref, wb_ref, *out_refs):
    acc = both_products(a_ref, b_ref, wa_ref, wb_ref)
    if half is None:
        scatter_rows(acc, out_refs, pieces)
        return
    j = pl.program_id(0)

    @pl.when(j < half)
    def _():
        scatter_rows(acc, out_refs[: len(pieces)], pieces)

    @pl.when(j >= half)
    def _():
        scatter_rows(acc, out_refs[len(pieces) :], pieces)


def project_call(kernel, operands, specs, out_shape, out_specs, count, tile, depth, name):
    rows = operands[0].shape[0]
    return pl.pallas_call(
        kernel,
        grid=(count // tile,),
        out_shape=out_shape,
        in_specs=specs,
        out_specs=out_specs,
        compiler_params=pltpu.CompilerParams(vmem_limit_bytes=VMEM_LIMIT),
        cost_estimate=pl.CostEstimate(
            flops=2 * rows * depth * count, bytes_accessed=2 * (depth + rows) * count, transcendentals=0
        ),
        name=name,
    )(*operands)


def weight_block(depth, first, tile):
    return pl.BlockSpec((depth, tile), lambda j: (0, j + first // tile))


def row_sizes(pieces):
    return [sum(stop - start for start, stop in spans) for spans in pieces]


def project_own(mine, weight, first, count, tile):
    rows, depth = mine.shape
    return project_call(
        own_kernel,
        (mine, stay(weight)),
        [pl.BlockSpec((rows, depth), lambda j: (0, 0)), weight_block(depth, first, tile)],
        jax.ShapeDtypeStruct((rows, count), jnp.float32),
        pl.BlockSpec((rows, tile), lambda j: (0, j)),
        count,
        tile,
        depth,
        "project_own",
    )


def project_rest(theirs, weight_pair, part, first, tile, pieces):
    rows, depth = theirs.shape
    count = part.shape[1]
    return project_call(
        functools.partial(rest_kernel, pieces),
        (theirs, stay(weight_pair), part),
        [
            pl.BlockSpec((rows, depth), lambda j: (0, 0)),
            weight_block(depth, first, tile),
            pl.BlockSpec((rows, tile), lambda j: (0, j)),
        ],
        [jax.ShapeDtypeStruct((n, count), jnp.bfloat16) for n in row_sizes(pieces)],
        [pl.BlockSpec((n, tile), lambda j: (0, j)) for n in row_sizes(pieces)],
        count,
        tile,
        depth,
        "project_rest",
    )


def project(mine, theirs, weight, weight_pair, first, count, tile, pieces, halves=False):
    rows, depth = mine.shape
    lhs = pl.BlockSpec((rows, depth), lambda j: (0, 0))
    rhs = weight_block(depth, first, tile)
    sizes = row_sizes(pieces)
    if halves:
        half = count // tile // 2
        shapes = [jax.ShapeDtypeStruct((n, count // 2), jnp.bfloat16) for n in sizes] * 2
        out_specs = [pl.BlockSpec((n, tile), lambda j: (0, jnp.minimum(j, half - 1))) for n in sizes]
        out_specs += [pl.BlockSpec((n, tile), lambda j: (0, jnp.maximum(j - half, 0))) for n in sizes]
    else:
        half = None
        shapes = [jax.ShapeDtypeStruct((n, count), jnp.bfloat16) for n in sizes]
        out_specs = [pl.BlockSpec((n, tile), lambda j: (0, j)) for n in sizes]
    return project_call(
        functools.partial(project_kernel, pieces, half),
        (mine, theirs, stay(weight), stay(weight_pair)),
        [lhs, lhs, rhs, rhs],
        shapes,
        out_specs,
        count,
        tile,
        2 * depth,
        "project",
    )


def moved(dy=0, dx=0, dc=0):
    pairs = []
    for y in range(N_Y):
        for x in range(N_X):
            for c in range(N_C):
                source = (y * N_X + x) * N_C + c
                target = (((y + dy) % N_Y) * N_X + (x + dx) % N_X) * N_C + (c + dc) % N_C
                pairs.append((source, target))
    return pairs


def send(array, **step):
    return lax.ppermute(array, "tp", moved(**step))


def add(*arrays):
    total = arrays[0].astype(jnp.float32)
    for array in arrays[1:]:
        total = total + array.astype(jnp.float32)
    return total


X_FIRST = (2304, 1280)


def body(queries, keys_in, values_in, short_taps, filters, skip_gain, out_weight, residual):
    rows = queries.shape[0]
    width = out_weight.shape[1]
    peers = lax.axis_size("ctx")
    piece = rows // (N_Y * N_X * N_C)
    weight_pair = send(out_weight, dc=1)
    rim = make_rim(queries, keys_in, values_in, short_taps)
    halo = lax.ppermute(rim, "ctx", [(i, i + 1) for i in range(peers - 1)])
    parameters = (short_taps, filters, skip_gain[None, :], transform_tables(filters.shape[1]))
    late, spec = gate_late(queries, keys_in, values_in, *parameters)
    place = lax.axis_index("tp").astype(jnp.int32)[None]
    keep, give = gate_early(place, queries, keys_in, values_in, halo, late, spec, short_taps, *parameters[2:])
    theirs = send(give, dc=1)

    half = rows // (2 * N_C)
    by_x = (((0, half),), ((half, 2 * half),))
    by_y = tuple(((s * piece, (s + 1) * piece), (half + s * piece, half + (s + 1) * piece)) for s in range(N_Y))

    def narrow(array):
        return array.astype(jnp.bfloat16)

    y_first = width - sum(X_FIRST)
    tile = y_first // 4
    a0_part = project_own(keep, out_weight, y_first, X_FIRST[0], tile)
    a0_keep, a0_give = project_rest(theirs, weight_pair, a0_part, y_first, tile, by_x)
    a0_got = send(a0_give, dx=1)
    left = lax.optimization_barrier((keep, a0_keep))[0]
    b_all = project(left, theirs, out_weight, weight_pair, 0, y_first, y_first // 2, by_y, halves=True)
    b0, b1 = b_all[:N_Y], b_all[N_Y:]
    left = lax.optimization_barrier((keep, b0[0]))[0]
    last = width - X_FIRST[1]
    a1_keep, a1_give = project(
        left, theirs, out_weight, weight_pair, last, X_FIRST[1], math.gcd(last, X_FIRST[1]), by_x
    )

    b1_far = send(b1[2], dy=1)
    b0_far = send(b0[2], dy=-1)
    b0_up = send(b0[1], dy=1)
    b1_down = send(b1[3], dy=-1)
    a1_got = send(lax.optimization_barrier((a1_give, a0_got))[0], dx=1)

    b0_far, b1_far, a0_got = lax.optimization_barrier((b0_far, b1_far, a0_got))
    b1_up = send(narrow(add(b1[1], b1_far)), dy=1)
    b0_down = send(narrow(add(b0[3], b0_far)), dy=-1)

    a0, a1 = add(a0_keep, a0_got), add(a1_keep, a1_got)
    edge = sum(X_FIRST) // 2
    low = [a0[s * piece : (s + 1) * piece, :edge] for s in range(N_Y)]
    high = [
        jnp.concatenate([a0[s * piece : (s + 1) * piece, edge:], a1[s * piece : (s + 1) * piece]], axis=1)
        for s in range(N_Y)
    ]
    low_send, high_send = [narrow(part) for part in low], [narrow(part) for part in high]
    low_send, high_send, b0_up, b1_down = lax.optimization_barrier((low_send, high_send, b0_up, b1_down))
    low_far = send(low_send[2], dy=-1)
    high_far = send(high_send[2], dy=1)

    b0_sum, b1_sum = add(b0[0], b0_up, b0_down), add(b1[0], b1_up, b1_down)
    b0_give, b1_give = narrow(b0_sum[piece:]), narrow(b1_sum[piece:])
    b0_got = send(b0_give, dx=1)

    low_far, high_far = lax.optimization_barrier((low_far, high_far))
    down = send(jnp.concatenate([narrow(add(low[3], low_far)), high_send[3]], axis=1), dy=-1)
    up = send(jnp.concatenate([low_send[1], narrow(add(high[1], high_far))], axis=1), dy=1)
    b1_got = send(lax.optimization_barrier((b1_give, low_far, high_far, b0_got))[0], dx=1)

    summed = jnp.concatenate(
        [
            add(b0_sum[:piece], b0_got),
            add(b1_sum[:piece], b1_got),
            add(jnp.concatenate([low[0], high[0]], axis=1), up, down),
        ],
        axis=1,
    )
    return narrow(residual.astype(jnp.float32) + summed)


def solution(mesh):
    in_specs = (
        P("ctx", "tp"),
        P("ctx", "tp"),
        P("ctx", "tp"),
        P(None, "tp"),
        P("tp", None),
        P("tp"),
        P("tp", None),
        P(("ctx", "tp"), None),
    )
    out_specs = P(("ctx", "tp"), None)
    return jax.shard_map(body, mesh=mesh, in_specs=in_specs, out_specs=out_specs, check_vma=False)
```
